32 devices in a mesh: dp: 2 (over y), row: 4 (over x, core), col: 4 (over z).
Axes of the slice: x: 2, y: 2, z: 4, core: 2. Of those that a mesh axis runs over, the one named last changes fastest.
Arguments:
- hidden_in: bfloat16 [4096, 1024], P(('dp', 'row'), 'col'), may hold values from -6 to 6
- segments: int32 [4096], P('dp'), may hold values from 0 to 15, never falling along the last dimension, each value on 1 to 800 neighbouring positions
- cotangent: bfloat16 [4096, 1024], P(('dp', 'row'), 'col'), may hold values from -6 to 6
- input_gain: float32 [2, 1024], P(None, 'col'), may hold values from 0.1 to 1.9
- query_weight: bfloat16 [2, 1024, 512], P(None, 'col', 'row'), may hold values from -0.1875 to 0.1875
- keyval_weight: bfloat16 [2, 1024, 256], P(None, 'col'), may hold values from -0.1875 to 0.1875
- mixer_gate_weight: bfloat16 [2, 1024, 1536], P(None, 'col', 'row'), may hold values from -0.1875 to 0.1875
- mixer_input_weight: bfloat16 [2, 1024, 1536], P(None, 'col', 'row'), may hold values from -0.1875 to 0.1875
- state_weight: bfloat16 [2, 1024, 256], P(None, 'col'), may hold values from -0.1875 to 0.1875
- step_weight: bfloat16 [2, 1024, 24], P(None, 'col'), may hold values from -0.1875 to 0.1875
- conv_values: float32 [2, 4, 1536], P(None, None, 'row'), may hold values from -3 to 3
- conv_shared: float32 [2, 4, 256], replicated, may hold values from -3 to 3
- step_bias: float32 [2, 24], P(None, 'row'), may hold values from -5 to -1
- decay_log: float32 [2, 24], P(None, 'row'), may hold values from -1.5 to 1.5
- skip_gain: float32 [2, 24], P(None, 'row'), may hold values from 0.5 to 2
- attention_out: bfloat16 [2, 512, 1024], P(None, 'row', 'col'), may hold values from -0.75 to 0.75
- mixer_out: bfloat16 [2, 1536, 1024], P(None, 'row', 'col'), may hold values from -0.15625 to 0.15625
- post_gain: float32 [2, 1024], P(None, 'col'), may hold values from 0.1 to 1.9
- gate_weight: bfloat16 [2, 1024, 2048], P(None, 'col', 'row'), may hold values from -0.1875 to 0.1875
- up_weight: bfloat16 [2, 1024, 2048], P(None, 'col', 'row'), may hold values from -0.1875 to 0.1875
- down_weight: bfloat16 [2, 2048, 1024], P(None, 'row', 'col'), may hold values from -0.125 to 0.125
Outputs:
- hidden_out: bfloat16 [4096, 1024], P(('dp', 'row'), 'col')
- hidden_grad: float32 [4096, 1024], P(('dp', 'row'), 'col')
- input_gain_grad: float32 [2, 1024], P(None, 'col')
- query_weight_grad: float32 [2, 1024, 512], P(None, 'col', 'row')
- keyval_weight_grad: float32 [2, 1024, 256], P(None, 'col')
- mixer_gate_weight_grad: float32 [2, 1024, 1536], P(None, 'col', 'row')
- mixer_input_weight_grad: float32 [2, 1024, 1536], P(None, 'col', 'row')
- state_weight_grad: float32 [2, 1024, 256], P(None, 'col')
- step_weight_grad: float32 [2, 1024, 24], P(None, 'col')
- conv_values_grad: float32 [2, 4, 1536], P(None, None, 'row')
- conv_shared_grad: float32 [2, 4, 256], replicated
- step_bias_grad: float32 [2, 24], P(None, 'row')
- decay_log_grad: float32 [2, 24], P(None, 'row')
- skip_gain_grad: float32 [2, 24], P(None, 'row')
- attention_out_grad: float32 [2, 512, 1024], P(None, 'row', 'col')
- mixer_out_grad: float32 [2, 1536, 1024], P(None, 'row', 'col')
- post_gain_grad: float32 [2, 1024], P(None, 'col')
- gate_weight_grad: float32 [2, 1024, 2048], P(None, 'col', 'row')
- up_weight_grad: float32 [2, 1024, 2048], P(None, 'col', 'row')
- down_weight_grad: float32 [2, 2048, 1024], P(None, 'row', 'col')
The draws below stay inside these ranges and needn't reach their ends.
Inputs may be any that keep to these rules, and one draw needn't show every extreme that they name: `segments`: document numbers never fall along the tokens; each document holds 800 tokens or fewer, and one holds exactly 800.
All inputs are finite; a program needn't handle non-finite values.
Results may differ from the reference program's by a relative error of at most 0.02.
Values may be sent and summed in bfloat16 or wider, within the bound.
No kernel may reach another device: no remote copies, remote signals or barrier semaphores. Data moves between devices by JAX's collectives and lax.ppermute only.
A program may use at most 192 MiB of HBM per device.

```python
import math
import jax
import jax.numpy as jnp
import numpy as np
from jax import lax

D = 1024
HEADS = 8
KV_HEADS = 2
HEAD = 64
M_HEADS = 24
M_HEAD = 64
STATE = 128
CONV = 4
FF = 2048
LAYERS = 2
SPAN = 128
TOK_DEV = 512
TOKENS = 4096
DOCS = 16
DOC_MOST = 800


def block_levels(rng, shape, shards, least, largest):
    factor_of, own = 1.0, jax.random.fold_in(rng, 6)
    for axis_at, shards_of in shards:
        heights = jnp.exp(jax.random.uniform(jax.random.fold_in(own, axis_at), (shards_of,), jnp.float32, least / len(shards), largest / len(shards)))
        factor_of = factor_of * jnp.repeat(heights, shape[axis_at] // shards_of).reshape([-1 if axis == axis_at else 1 for axis in range(len(shape))])
    return factor_of


def split_up(amount, total, bound, lean):
    weights = [(1 << 20) // math.isqrt(standing ** lean) + 1 for standing in range(2, amount + 1)]
    surplus, counts = total - bound - (amount - 1), [1] * (amount - 1)
    while surplus > 0:
        free = [i for i in range(amount - 1) if counts[i] < bound]
        whole, remaining = sum([weights[i] for i in free]), surplus
        for i in free:
            extra = min(bound - counts[i], max(1, remaining * weights[i] // whole), surplus)
            counts[i] = counts[i] + extra
            surplus = surplus - extra
    return np.array([bound] + counts)


def ragged(stream_key, amount, total, limit, lean):
    if amount == 2:
        one = jax.random.randint(stream_key, (), max(1, total - limit), min(limit, total - 1) + 1)
        return jnp.stack([one, total - one])
    sizes = jnp.asarray(split_up(amount, total, limit, lean), jnp.int32)
    twos = (amount - 1) // 2
    donor, taker = sizes[1:1 + 2 * twos:2], sizes[2:2 + 2 * twos:2]
    slack = jnp.minimum(donor - 1, limit - taker)
    shifted = jax.random.randint(jax.random.fold_in(stream_key, 1), (twos,), 0, 1 << 20) % (slack + 1)
    sizes = sizes.at[1:1 + 2 * twos:2].set(donor - shifted).at[2:2 + 2 * twos:2].set(taker + shifted)
    return sizes[jax.random.permutation(jax.random.fold_in(stream_key, 2), amount)]


def scatter_about(own_key, dims, scale, limit, shards=(), kind=jnp.bfloat16):
    level = block_levels(own_key, dims, shards, -0.22, 0.18) if shards else 1.0
    values = jax.random.normal(own_key, dims, jnp.float32) * scale * level
    return jnp.minimum(jnp.maximum(values, -limit), limit).astype(kind)


def setup_inputs(seed: int = 0) -> dict:
    streams_of = jax.random.split(jax.random.key(seed), 22)
    return {
        "hidden_in": scatter_about(streams_of[0], (TOKENS, D), 1.0, 6.0, ((0, 8), (1, 4))),
        "segments": jnp.searchsorted(jnp.cumsum(ragged(streams_of[1], DOCS, TOKENS, DOC_MOST, 1)), jnp.arange(TOKENS), side="right").astype(jnp.int32),
        "cotangent": scatter_about(streams_of[2], (TOKENS, D), 1.0, 6.0, ((0, 8), (1, 4))),
        "input_gain": jnp.clip(1.0 + 0.18 * jax.random.normal(streams_of[3], (LAYERS, D), jnp.float32), 0.1, 1.9),
        "query_weight": scatter_about(streams_of[4], (LAYERS, D, HEADS * HEAD), D ** -0.5, 0.1875, ((1, 4), (2, 4))),
        "keyval_weight": scatter_about(streams_of[5], (LAYERS, D, 2 * KV_HEADS * HEAD), D ** -0.5, 0.1875, ((1, 4),)),
        "mixer_gate_weight": scatter_about(streams_of[6], (LAYERS, D, M_HEADS * M_HEAD), D ** -0.5, 0.1875, ((1, 4), (2, 4))),
        "mixer_input_weight": scatter_about(streams_of[7], (LAYERS, D, M_HEADS * M_HEAD), D ** -0.5, 0.1875, ((1, 4), (2, 4))),
        "state_weight": scatter_about(streams_of[8], (LAYERS, D, 2 * STATE), D ** -0.5, 0.1875, ((1, 4),)),
        "step_weight": scatter_about(streams_of[9], (LAYERS, D, M_HEADS), D ** -0.5, 0.1875, ((1, 4),)),
        "conv_values": scatter_about(streams_of[10], (LAYERS, CONV, M_HEADS * M_HEAD), 0.5, 3.0, ((2, 4),), jnp.float32),
        "conv_shared": scatter_about(streams_of[11], (LAYERS, CONV, 2 * STATE), 0.5, 3.0, (), jnp.float32),
        "step_bias": jnp.clip(-5.0 + 4.0 * jax.random.uniform(streams_of[12], (LAYERS, M_HEADS), jnp.float32) ** block_levels(streams_of[12], (LAYERS, M_HEADS), ((1, 4),), -0.2, 0.2), -5.0, -1.0),
        "decay_log": jnp.clip(jax.random.uniform(streams_of[13], (LAYERS, M_HEADS), jnp.float32, -1.5, 1.5) * block_levels(streams_of[13], (LAYERS, M_HEADS), ((1, 4),), -0.4, 0.0), -1.5, 1.5),
        "skip_gain": jnp.clip(0.5 + 1.5 * jax.random.uniform(streams_of[14], (LAYERS, M_HEADS), jnp.float32) ** block_levels(streams_of[14], (LAYERS, M_HEADS), ((1, 4),), -0.2, 0.2), 0.5, 2.0),
        "attention_out": scatter_about(streams_of[15], (LAYERS, HEADS * HEAD, D), (HEADS * HEAD // 8) ** -0.5, 0.75, ((1, 4), (2, 4))),
        "mixer_out": scatter_about(streams_of[16], (LAYERS, M_HEADS * M_HEAD, D), (M_HEADS * M_HEAD) ** -0.5, 0.15625, ((1, 4), (2, 4))),
        "post_gain": jnp.clip(1.0 + 0.18 * jax.random.normal(streams_of[17], (LAYERS, D), jnp.float32), 0.1, 1.9),
        "gate_weight": scatter_about(streams_of[18], (LAYERS, D, FF), D ** -0.5, 0.1875, ((1, 4), (2, 4))),
        "up_weight": scatter_about(streams_of[19], (LAYERS, D, FF), D ** -0.5, 0.1875, ((1, 4), (2, 4))),
        "down_weight": scatter_about(streams_of[20], (LAYERS, FF, D), FF ** -0.5, 0.125, ((1, 4), (2, 4))),
    }


epsilon = 1e-05
highest = lax.Precision.HIGHEST

@jax.custom_vjp
def low(v):
    return lax.optimization_barrier(v.astype(jnp.bfloat16)).astype(jnp.float32)

@jax.custom_vjp
def low_back(v):
    return v

def low_keep(v):
    return (low(v), None)

def low_pass(kept, grad):
    return (grad,)

def back_keep(v):
    return (v, None)

def back_low(kept, grad):
    return (low(grad),)
low.defvjp(low_keep, low_pass)
low_back.defvjp(back_keep, back_low)

def exact_dot(left, right):
    return jnp.dot(left, right, precision=highest)

def rms_norm(hidden, gain):
    return hidden * lax.rsqrt(lax.optimization_barrier(jnp.mean(hidden * hidden, axis=-1, keepdims=True)) + epsilon) * gain

def causal_conv(signal, kernel, segment_ids):
    length = signal.shape[0]
    summed = signal * kernel[0][None, :]
    for offset in range(1, kernel.shape[0]):
        earlier = jnp.concatenate([jnp.zeros((offset, signal.shape[1]), signal.dtype), signal[:length - offset]], axis=0)
        prior_ids = jnp.concatenate([jnp.full((offset,), -1, jnp.int32), segment_ids[:length - offset].astype(jnp.int32)])
        same_doc = (prior_ids == segment_ids.astype(jnp.int32)).astype(signal.dtype)
        summed = summed + earlier * kernel[offset][None, :] * same_doc[:, None]
    return summed

def attend(queries, key_heads, value_heads, segment_ids):
    length, query_count, head_size = queries.shape
    kv_count = key_heads.shape[1]
    block_rows = min(512, length)
    positions = jnp.arange(length, dtype=jnp.int32)
    scaling = head_size ** (-0.5)

    def query_block(block_index):
        first_row = block_index * block_rows
        chosen = lax.dynamic_slice_in_dim(queries, first_row, block_rows, 0)
        chosen = chosen.reshape(block_rows, kv_count, query_count // kv_count, head_size)
        query_pos = first_row + jnp.arange(block_rows, dtype=jnp.int32)
        query_seg = lax.dynamic_slice_in_dim(segment_ids, first_row, block_rows, 0)
        scores = jnp.einsum('qkge,ske->kgqs', chosen, key_heads, precision=highest) * scaling
        allowed = (query_pos[:, None] >= positions[None, :]) & (query_seg[:, None] == segment_ids[None, :])
        scores = jnp.where(allowed[None, None], scores, -1e+30)
        highest_score = lax.optimization_barrier(jnp.max(scores, axis=-1, keepdims=True))
        weights = jnp.exp(scores - highest_score)
        weights_low = low(weights / lax.optimization_barrier(jnp.sum(weights, axis=-1, keepdims=True)))
        attended = jnp.einsum('kgqs,ske->qkge', weights_low, value_heads, precision=highest)
        return attended.reshape(block_rows, query_count * head_size)
    blocks = lax.map(jax.checkpoint(query_block), jnp.arange(length // block_rows, dtype=jnp.int32))
    return blocks.reshape(length, query_count * head_size)

def scan_spans(inner, bmatrix, cmatrix, time_steps, rates, segment_ids, width):
    length, head_count, head_size = inner.shape
    span_count = length // width
    state_size = bmatrix.shape[1]
    seg_blocks = segment_ids.astype(jnp.int32).reshape(span_count, width)
    previous = jnp.concatenate([jnp.full((1,), -1, jnp.int32), seg_blocks[:-1, -1]])
    positions = jnp.arange(width, dtype=jnp.int32)
    causal = positions[:, None] >= positions[None, :]

    def span_step(carry_state, pieces):
        block_inner, block_b, block_c, block_dt, block_seg, prior_segment = pieces
        cumulative = jnp.cumsum(-block_dt * rates[None, :], axis=0)
        inside = causal & (block_seg[:, None] == block_seg[None, :])
        spread = jnp.where(inside[:, :, None], cumulative[:, None, :] - cumulative[None, :, :], 0.0)
        decay_matrix = jnp.exp(spread) * inside[:, :, None].astype(cumulative.dtype)
        affinity = jnp.dot(block_c, block_b.T, precision=highest)
        scaled = block_inner * block_dt[:, :, None]
        result = jnp.einsum('ijh,jhp->ihp', affinity[:, :, None] * decay_matrix, scaled, precision=highest)
        continuing = (block_seg == prior_segment).astype(cumulative.dtype)
        carried = jnp.einsum('in,hpn->ihp', block_c, carry_state, precision=highest)
        result = result + carried * (jnp.exp(cumulative) * continuing[:, None])[:, :, None]
        last_segment = block_seg[-1]
        tail_weight = jnp.exp(cumulative[-1][None, :] - cumulative) * (block_seg == last_segment).astype(cumulative.dtype)[:, None]
        retained = jnp.exp(cumulative[-1]) * (last_segment == prior_segment).astype(cumulative.dtype)
        update = jnp.einsum('jhp,jn->hpn', scaled * tail_weight[:, :, None], block_b, precision=highest)
        return (carry_state * retained[:, None, None] + update, result)
    zero_state = jnp.zeros((head_count, head_size, state_size), inner.dtype)
    pieces = (inner.reshape(span_count, width, head_count, head_size), bmatrix.reshape(span_count, width, state_size), cmatrix.reshape(span_count, width, state_size), time_steps.reshape(span_count, width, head_count), seg_blocks, previous)
    ignored, outputs = lax.scan(jax.checkpoint(span_step), zero_state, pieces)
    return outputs.reshape(length, head_count, head_size)

def mixer_heads(queries, keyval, mgate, minput, states, time_raw, segment_ids, conv_values, conv_shared, step_bias, decay_log, skip_gain, kv_count, head_size, mamba_size, width):
    length = queries.shape[0]
    query_heads = low(queries).reshape(length, -1, head_size)
    keyval_low = low(keyval)
    key_heads = keyval_low[:, :kv_count * head_size].reshape(length, kv_count, head_size)
    value_heads = keyval_low[:, kv_count * head_size:].reshape(length, kv_count, head_size)
    attended = low(attend(query_heads, key_heads, value_heads, segment_ids))
    inner = jax.nn.silu(causal_conv(minput, conv_values, segment_ids))
    shared = jax.nn.silu(causal_conv(states, conv_shared, segment_ids))
    half_width = shared.shape[1] // 2
    head_count = time_raw.shape[1]
    time_steps = jax.nn.softplus(time_raw + step_bias[None, :])
    inner_heads = inner.reshape(length, head_count, mamba_size)
    scanned = scan_spans(inner_heads, shared[:, :half_width], shared[:, half_width:], time_steps, jnp.exp(decay_log), segment_ids, width)
    scanned = scanned + skip_gain[None, :, None] * inner_heads
    mamba = low(scanned.reshape(length, head_count * mamba_size) * jax.nn.silu(mgate))
    return (attended, mamba)

def layer_forward(hidden, segment_ids, params):
    input_gain, query_weight, keyval_weight, mixer_gate_weight, mixer_input_weight, state_weight, step_weight, conv_values, conv_shared, step_bias, decay_log, skip_gain, attention_out, mixer_out, post_gain, gate_weight, up_weight, down_weight = params
    normed = low(rms_norm(hidden, input_gain))
    queries = low_back(exact_dot(normed, query_weight))
    keyval = low_back(exact_dot(normed, keyval_weight))
    mgate = low_back(exact_dot(normed, mixer_gate_weight))
    minput = low_back(exact_dot(normed, mixer_input_weight))
    states = low_back(exact_dot(normed, state_weight))
    time_raw = low_back(exact_dot(normed, step_weight))
    seq_count = hidden.shape[0] // TOK_DEV

    def sequence(pieces):
        return mixer_heads(pieces[0], pieces[1], pieces[2], pieces[3], pieces[4], pieces[5], pieces[6], conv_values, conv_shared, step_bias, decay_log, skip_gain, KV_HEADS, HEAD, M_HEAD, SPAN)

    def sequence_blocks(array):
        return array.reshape((seq_count, TOK_DEV) + array.shape[1:])
    attended, mamba = lax.map(jax.checkpoint(sequence), (sequence_blocks(queries), sequence_blocks(keyval), sequence_blocks(mgate), sequence_blocks(minput), sequence_blocks(states), sequence_blocks(time_raw), sequence_blocks(segment_ids)))
    attended = attended.reshape(hidden.shape[0], -1)
    mamba = mamba.reshape(hidden.shape[0], -1)
    branch = low_back(exact_dot(attended, attention_out) + exact_dot(mamba, mixer_out))
    middle = hidden + branch
    post_normed = low(rms_norm(middle, post_gain))
    gate = low_back(exact_dot(post_normed, gate_weight))
    upper = low_back(exact_dot(post_normed, up_weight))
    activated = low(jax.nn.silu(gate) * upper)
    return middle + low_back(exact_dot(activated, down_weight))

def reference(hidden_in, segments, cotangent, input_gain, query_weight, keyval_weight, mixer_gate_weight, mixer_input_weight, state_weight, step_weight, conv_values, conv_shared, step_bias, decay_log, skip_gain, attention_out, mixer_out, post_gain, gate_weight, up_weight, down_weight):
    weights = tuple((stacked.astype(jnp.float32) for stacked in (input_gain, query_weight, keyval_weight, mixer_gate_weight, mixer_input_weight, state_weight, step_weight, conv_values, conv_shared, step_bias, decay_log, skip_gain, attention_out, mixer_out, post_gain, gate_weight, up_weight, down_weight)))

    def forward(hidden, *params):
        for layer_index in range(LAYERS):
            hidden = layer_forward(hidden, segments, tuple((stacked[layer_index] for stacked in params)))
        return hidden
    output, pullback = jax.vjp(forward, hidden_in.astype(jnp.float32), *weights)
    gradients = pullback(cotangent.astype(jnp.float32))
    return (output.astype(jnp.bfloat16), gradients[0], gradients[1], gradients[2], gradients[3], gradients[4], gradients[5], gradients[6], gradients[7], gradients[8], gradients[9], gradients[10], gradients[11], gradients[12], gradients[13], gradients[14], gradients[15], gradients[16], gradients[17], gradients[18])
```

```python
from functools import partial

import jax
import jax.numpy as jnp
from jax import lax
from jax.experimental import pallas as pl
from jax.experimental.pallas import tpu as pltpu
from jax.sharding import PartitionSpec as P

HEADS = 8
KV_HEADS = 2
HEAD = 64
M_HEAD = 64
LAYERS = 2
LANES = 128
ROWS = 128

epsilon = 1e-05
highest = lax.Precision.HIGHEST
f32 = jnp.float32
bf16 = jnp.bfloat16

NN = (((1,), (0,)), ((), ()))
NT = (((1,), (1,)), ((), ()))
TN = (((0,), (0,)), ((), ()))


def dot(left, right, dims=NN, precision=None):
    return lax.dot_general(left, right, dims, precision=precision, preferred_element_type=f32)


def left_lanes():
    return lax.broadcasted_iota(jnp.int32, (ROWS, LANES), 1) < HEAD


def side_lanes():
    lane = lax.broadcasted_iota(jnp.int32, (ROWS, LANES), 1)
    return lane < HEAD, lane >= HEAD


def prepare(block, sizes, proj_ref, link_ref, taps_ref, heads_ref, spread_ref):
    first, last = block * ROWS, (block + 1) * ROWS
    conv_first, conv_last, steps_first = sizes[2], sizes[4], sizes[5]
    signal = proj_ref[first:last, conv_first:conv_last]
    if block == 0:
        prior = jnp.zeros((8, conv_last - conv_first), f32)
    else:
        prior = proj_ref[first - 8 : first, conv_first:conv_last]
    joined = jnp.concatenate([prior, signal], axis=0)
    pre = signal * taps_ref[0:1, :]
    for offset in range(1, 4):
        earlier = joined[8 - offset : 8 - offset + ROWS]
        pre = pre + earlier * taps_ref[offset : offset + 1, :] * link_ref[first:last, offset : offset + 1]
    raw = proj_ref[first:last, steps_first : steps_first + LANES] + heads_ref[0:1, :]
    steps = jnp.maximum(raw, 0.0) + jnp.log1p(jnp.exp(-jnp.abs(raw)))
    wide = dot(steps, spread_ref[...], NN, highest)
    return pre, raw, steps, wide


def running(steps, heads_ref, carry):
    lower = (
        lax.broadcasted_iota(jnp.int32, (ROWS, ROWS), 0)
        >= lax.broadcasted_iota(jnp.int32, (ROWS, ROWS), 1)
    ).astype(f32)
    return dot(lower, -steps * heads_ref[1:2, :], NN, highest) + carry


def key_value(block, sizes, proj_ref):
    pair = proj_ref[block * ROWS : (block + 1) * ROWS, sizes[4] : sizes[5]]
    turned = pltpu.roll(pair, HEAD, 1)
    left = left_lanes()
    return jnp.where(left, pair, turned).astype(bf16), jnp.where(left, turned, pair).astype(bf16)


def hidden_links(block, segc_ref, segr_ref):
    width = (block + 1) * ROWS
    token = lax.broadcasted_iota(jnp.int32, (ROWS, width), 0) + block * ROWS
    source = lax.broadcasted_iota(jnp.int32, (ROWS, width), 1)
    same = segc_ref[block * ROWS : width, :] == segr_ref[:, :width]
    return jnp.where((token >= source) & same, 0.0, -1e30)


def mixer_forward_kernel(
    sizes,
    proj_ref,
    segc_ref,
    segr_ref,
    link_ref,
    taps_ref,
    heads_ref,
    skip_ref,
    spread_ref,
    out_ref,
    inner_s,
    xdt_s,
    b_s,
    c_s,
    cum_s,
    turned_s,
    key_s,
    value_s,
):
    blocks = proj_ref.shape[0] // ROWS
    width = sizes[3] - sizes[2]
    carry = jnp.zeros((1, LANES), f32)
    for block in range(blocks):
        rows = slice(block * ROWS, (block + 1) * ROWS)
        pre, raw, steps, wide = prepare(
            block, sizes, proj_ref, link_ref, taps_ref, heads_ref, spread_ref
        )
        active = pre * jax.nn.sigmoid(pre)
        inner = active[:, :width]
        inner_s[rows, :] = inner
        xdt_s[rows, :] = (inner * wide).astype(bf16)
        b_s[rows, :] = active[:, width : width + LANES].astype(bf16)
        c_s[rows, :] = active[:, width + LANES :].astype(bf16)
        cum = running(steps, heads_ref, carry)
        carry = cum[ROWS - 1 :, :]
        cum_s[rows, :] = cum
        turned_s[:, rows] = cum.T
        key_s[rows, :], value_s[rows, :] = key_value(block, sizes, proj_ref)
    left = left_lanes()
    for block in range(blocks):
        rows = slice(block * ROWS, (block + 1) * ROWS)
        span = (block + 1) * ROWS
        bias = hidden_links(block, segc_ref, segr_ref)
        query = proj_ref[rows, : sizes[1]]
        parts = []
        for side in range(2):
            chosen = jnp.where(side_lanes()[side], query, 0.0).astype(bf16)
            scores = dot(chosen, key_s[:span, :], NT) * (HEAD**-0.5) + bias
            weights = jnp.exp(scores - jnp.max(scores, axis=1, keepdims=True))
            weights = weights * (1.0 / jnp.sum(weights, axis=1, keepdims=True))
            parts.append(dot(weights.astype(bf16), value_s[:span, :]))
        out_ref[rows, : sizes[1]] = jnp.where(left, parts[0], parts[1]).astype(bf16)
        affinity = dot(c_s[rows, :], b_s[:span, :], NT)
        for pair in range(width // LANES):
            cols = slice(pair * LANES, (pair + 1) * LANES)
            parts = []
            for side in range(2):
                head = 2 * pair + side
                decay = jnp.exp(
                    cum_s[rows, head : head + 1] - turned_s[head : head + 1, :span] + bias
                )
                parts.append(dot((affinity * decay).astype(bf16), xdt_s[:span, cols]))
            scanned = jnp.where(left, parts[0], parts[1])
            scanned = scanned + skip_ref[:, cols] * inner_s[rows, cols]
            gate = proj_ref[rows, sizes[1] + pair * LANES : sizes[1] + (pair + 1) * LANES]
            out_ref[rows, sizes[1] + pair * LANES : sizes[1] + (pair + 1) * LANES] = (
                scanned * gate * jax.nn.sigmoid(gate)
            ).astype(bf16)


def mixer_backward_kernel(
    sizes,
    proj_ref,
    dmix_ref,
    segc_ref,
    segr_ref,
    link_ref,
    taps_ref,
    heads_ref,
    skip_ref,
    spread_ref,
    dproj_ref,
    dtaps_ref,
    dheads_ref,
    inner_s,
    xdt_s,
    b_s,
    c_s,
    cum_s,
    turned_s,
    key_s,
    value_s,
    pre_s,
    dscan_s,
    dxdt_s,
    db_s,
    dc_s,
    dkey_s,
    dvalue_s,
    dcum_s,
    dpre_s,
):
    length = proj_ref.shape[0]
    blocks = length // ROWS
    width = sizes[3] - sizes[2]
    conv_first, conv_last, steps_first = sizes[2], sizes[4], sizes[5]
    conv_width = conv_last - conv_first
    carry = jnp.zeros((1, LANES), f32)
    for block in range(blocks):
        rows = slice(block * ROWS, (block + 1) * ROWS)
        pre, raw, steps, wide = prepare(
            block, sizes, proj_ref, link_ref, taps_ref, heads_ref, spread_ref
        )
        pre_s[rows, :] = pre
        active = pre * jax.nn.sigmoid(pre)
        inner = active[:, :width]
        inner_s[rows, :] = inner
        xdt_s[rows, :] = (inner * wide).astype(bf16)
        b_s[rows, :] = active[:, width : width + LANES].astype(bf16)
        c_s[rows, :] = active[:, width + LANES :].astype(bf16)
        cum = running(steps, heads_ref, carry)
        carry = cum[ROWS - 1 :, :]
        cum_s[rows, :] = cum
        turned_s[:, rows] = cum.T
        key_s[rows, :], value_s[rows, :] = key_value(block, sizes, proj_ref)
    dxdt_s[...] = jnp.zeros_like(dxdt_s)
    db_s[...] = jnp.zeros_like(db_s)
    dkey_s[...] = jnp.zeros_like(dkey_s)
    dvalue_s[...] = jnp.zeros_like(dvalue_s)
    left = left_lanes()
    dskip = jnp.zeros((1, width), f32)
    for block in range(blocks):
        rows = slice(block * ROWS, (block + 1) * ROWS)
        span = (block + 1) * ROWS
        bias = hidden_links(block, segc_ref, segr_ref)
        query = proj_ref[rows, : sizes[1]]
        dattended = dmix_ref[rows, : sizes[1]]
        parts = []
        for side in range(2):
            own = side_lanes()[side]
            chosen = jnp.where(own, query, 0.0).astype(bf16)
            dchosen = jnp.where(own, dattended, 0.0).astype(bf16)
            scores = dot(chosen, key_s[:span, :], NT) * (HEAD**-0.5) + bias
            weights = jnp.exp(scores - jnp.max(scores, axis=1, keepdims=True))
            weights = weights * (1.0 / jnp.sum(weights, axis=1, keepdims=True))
            dweights = dot(dchosen, value_s[:span, :], NT)
            dvalue_s[:span, :] += dot(weights.astype(bf16), dchosen, TN)
            mean = jnp.sum(weights * dweights, axis=1, keepdims=True)
            dscores = (weights * (dweights - mean) * (HEAD**-0.5)).astype(bf16)
            parts.append(dot(dscores, key_s[:span, :]))
            dkey_s[:span, :] += dot(dscores, chosen, TN)
        dproj_ref[rows, : sizes[1]] = jnp.where(left, parts[0], parts[1]).astype(bf16)
        affinity = dot(c_s[rows, :], b_s[:span, :], NT)
        daffinity = jnp.zeros((ROWS, span), f32)
        dcum = jnp.zeros((ROWS, LANES), f32)
        for pair in range(width // LANES):
            cols = slice(pair * LANES, (pair + 1) * LANES)
            gate_cols = slice(sizes[1] + pair * LANES, sizes[1] + (pair + 1) * LANES)
            gate = proj_ref[rows, gate_cols]
            lifted = jax.nn.sigmoid(gate)
            dmamba = dmix_ref[rows, gate_cols]
            dscan = dmamba * gate * lifted
            dscan_s[rows, cols] = dscan
            parts, mixes, sides = [], [], []
            for side in range(2):
                head = 2 * pair + side
                decay = jnp.exp(
                    cum_s[rows, head : head + 1] - turned_s[head : head + 1, :span] + bias
                )
                mix = (affinity * decay).astype(bf16)
                dside = jnp.where(side_lanes()[side], dscan, 0.0).astype(bf16)
                daffinity = daffinity + dot(dside, xdt_s[:span, cols], NT) * decay
                parts.append(dot(mix, xdt_s[:span, cols]))
                mixes.append(mix)
                sides.append(dside)
            dxdt_s[:span, cols] += dot(
                jnp.concatenate(mixes, axis=0), jnp.concatenate(sides, axis=0), TN
            )
            scanned = jnp.where(left, parts[0], parts[1])
            inner = inner_s[rows, cols]
            dcum = dcum + dot(
                scanned * dscan.astype(bf16).astype(f32), spread_ref[:, cols], NT, highest
            )
            scanned = scanned + skip_ref[:, cols] * inner
            dproj_ref[rows, gate_cols] = (
                dmamba * scanned * lifted * (1.0 + gate * (1.0 - lifted))
            ).astype(bf16)
        dcum_s[rows, :] = dcum
        dskip = dskip + jnp.sum(dscan_s[rows, :] * inner_s[rows, :], axis=0, keepdims=True)
        daffinity = daffinity.astype(bf16)
        dc_s[rows, :] = dot(daffinity, b_s[:span, :])
        db_s[:span, :] += dot(daffinity, c_s[rows, :], TN)
    upper = (
        lax.broadcasted_iota(jnp.int32, (ROWS, ROWS), 0)
        <= lax.broadcasted_iota(jnp.int32, (ROWS, ROWS), 1)
    ).astype(f32)
    carry = jnp.zeros((1, LANES), f32)
    dbias = jnp.zeros((1, LANES), f32)
    drate = jnp.zeros((1, LANES), f32)
    dpre_s[length:, :] = jnp.zeros((8, conv_width), f32)
    for block in reversed(range(blocks)):
        rows = slice(block * ROWS, (block + 1) * ROWS)
        raw = proj_ref[rows, steps_first : steps_first + LANES] + heads_ref[0:1, :]
        steps = jnp.maximum(raw, 0.0) + jnp.log1p(jnp.exp(-jnp.abs(raw)))
        wide = dot(steps, spread_ref[...], NN, highest)
        dxdt = dxdt_s[rows, :]
        dcum = dcum_s[rows, :] - dot(
            xdt_s[rows, :].astype(f32) * dxdt, spread_ref[...], NT, highest
        )
        dlog = dot(upper, dcum, NN, highest) + carry
        carry = dlog[0:1, :]
        dsteps = (
            dot(dxdt * inner_s[rows, :], spread_ref[...], NT, highest) - heads_ref[1:2, :] * dlog
        )
        drate = drate - jnp.sum(steps * dlog, axis=0, keepdims=True)
        draw = dsteps * jax.nn.sigmoid(raw)
        dbias = dbias + jnp.sum(draw, axis=0, keepdims=True)
        dproj_ref[rows, steps_first : steps_first + LANES] = draw.astype(bf16)
        dinner = dxdt * wide + skip_ref[...] * dscan_s[rows, :]
        dactive = jnp.concatenate([dinner, db_s[rows, :], dc_s[rows, :]], axis=1)
        pre = pre_s[rows, :]
        lifted = jax.nn.sigmoid(pre)
        dpre_s[rows, :] = dactive * lifted * (1.0 + pre * (1.0 - lifted))
        dkey = dkey_s[rows, :]
        dvalue = dvalue_s[rows, :]
        dkey = dkey + pltpu.roll(dkey, HEAD, 1)
        dvalue = dvalue + pltpu.roll(dvalue, HEAD, 1)
        dproj_ref[rows, conv_last:steps_first] = jnp.where(left, dkey, dvalue).astype(bf16)
    dtaps = [jnp.zeros((1, conv_width), f32) for _ in range(4)]
    for block in range(blocks):
        first, last = block * ROWS, (block + 1) * ROWS
        signal = proj_ref[first:last, conv_first:conv_last]
        joined = dpre_s[first : last + 8, :]
        own = joined[:ROWS]
        dsignal = own * taps_ref[0:1, :]
        dtaps[0] = dtaps[0] + jnp.sum(signal * own, axis=0, keepdims=True)
        for offset in range(1, 4):
            later = (joined * link_ref[first : last + 8, offset : offset + 1])[
                offset : offset + ROWS
            ]
            dsignal = dsignal + later * taps_ref[offset : offset + 1, :]
            dtaps[offset] = dtaps[offset] + jnp.sum(signal * later, axis=0, keepdims=True)
        dproj_ref[first:last, conv_first:conv_last] = dsignal.astype(bf16)
    dtaps_ref[...] = jnp.concatenate(dtaps + [jnp.zeros((4, conv_width), f32)], axis=0)
    dheads_ref[...] = jnp.concatenate(
        [
            dbias,
            drate * heads_ref[1:2, :],
            dot(dskip, spread_ref[...], NT, highest),
            jnp.zeros((5, LANES), f32),
        ],
        axis=0,
    )


def shared_scratch(length, width):
    return [
        pltpu.VMEM((length, width), f32),
        pltpu.VMEM((length, width), bf16),
        pltpu.VMEM((length, LANES), bf16),
        pltpu.VMEM((length, LANES), bf16),
        pltpu.VMEM((length, LANES), f32),
        pltpu.VMEM((LANES, length), f32),
        pltpu.VMEM((length, LANES), bf16),
        pltpu.VMEM((length, LANES), bf16),
    ]


def mixer_forward(sizes, proj, side):
    length, width = proj.shape[0], sizes[3] - sizes[2]
    return pl.pallas_call(
        partial(mixer_forward_kernel, sizes),
        out_shape=jax.ShapeDtypeStruct((length, sizes[2]), bf16),
        scratch_shapes=shared_scratch(length, width),
        compiler_params=pltpu.CompilerParams(vmem_limit_bytes=40 * 1024 * 1024),
        cost_estimate=pl.CostEstimate(flops=10**9, bytes_accessed=4 * 10**6, transcendentals=10**6),
        name="mixer_forward",
    )(proj, *side)


def mixer_backward(sizes, proj, dmix, side):
    length, width = proj.shape[0], sizes[3] - sizes[2]
    conv_width = sizes[4] - sizes[2]
    return pl.pallas_call(
        partial(mixer_backward_kernel, sizes),
        out_shape=(
            jax.ShapeDtypeStruct(proj.shape, bf16),
            jax.ShapeDtypeStruct((8, conv_width), f32),
            jax.ShapeDtypeStruct((8, LANES), f32),
        ),
        scratch_shapes=shared_scratch(length, width)
        + [
            pltpu.VMEM((length, conv_width), f32),
            pltpu.VMEM((length, width), f32),
            pltpu.VMEM((length, width), f32),
            pltpu.VMEM((length, LANES), f32),
            pltpu.VMEM((length, LANES), f32),
            pltpu.VMEM((length, LANES), f32),
            pltpu.VMEM((length, LANES), f32),
            pltpu.VMEM((length, LANES), f32),
            pltpu.VMEM((length + 8, conv_width), f32),
        ],
        compiler_params=pltpu.CompilerParams(vmem_limit_bytes=48 * 1024 * 1024),
        cost_estimate=pl.CostEstimate(flops=3 * 10**9, bytes_accessed=6 * 10**6, transcendentals=10**6),
        name="mixer_backward",
    )(proj, dmix, *side)


def swap(value, distance):
    size = lax.axis_size("row")
    return lax.ppermute(value, "row", [(i, i ^ distance) for i in range(size)])


def row_sum(part):
    if lax.axis_size("row") != 4:
        return lax.psum(part, "row")
    half = part.shape[0] // 2
    parity = lax.axis_index("row") % 2
    away = lax.dynamic_slice_in_dim(part, (1 - parity) * half, half, 0)
    kept = lax.dynamic_slice_in_dim(part, parity * half, half, 0)
    kept = (kept.astype(f32) + swap(away, 1).astype(f32)).astype(bf16)
    kept = (kept.astype(f32) + swap(kept, 2).astype(f32)).astype(bf16)
    other = swap(kept, 1)
    return jnp.where(
        parity == 0,
        jnp.concatenate([kept, other], axis=0),
        jnp.concatenate([other, kept], axis=0),
    )


def transpose_blocks(value):
    rows, cols = lax.axis_size("row"), lax.axis_size("col")
    pairs = [(r * cols + c, c * cols + r) for r in range(rows) for c in range(cols)]
    return lax.ppermute(value, ("row", "col"), pairs)


def whole_features(value):
    return lax.all_gather(transpose_blocks(value), "row", axis=1, tiled=True)


def own_block(value):
    count = value.shape[1] // lax.axis_size("row")
    block = lax.dynamic_slice_in_dim(value, lax.axis_index("row") * count, count, 1)
    return transpose_blocks(block)


def gather_weight(weight):
    return lax.all_gather(weight, "col", axis=0, tiled=True)


def scatter_grad(grad):
    grad = lax.psum_scatter(grad.astype(bf16), "col", scatter_dimension=0, tiled=True)
    return lax.psum(grad, "dp")


def norm(hidden, gain):
    inverse = lax.rsqrt(jnp.mean(hidden * hidden, axis=1, keepdims=True) + epsilon)
    return (hidden * inverse * gain[None, :]).astype(bf16), inverse


def norm_back(hidden, inverse, gain, grad):
    weighted = grad * gain[None, :]
    mean = jnp.mean(weighted * hidden, axis=1, keepdims=True)
    grad_hidden = inverse * weighted - hidden * (inverse * inverse * inverse * mean)
    return grad_hidden, jnp.sum(grad * hidden * inverse, axis=0)


def layer_forward(hidden, params, sizes):
    input_gain, post_gain, in_weight, out_weight, ffn_weight, side = params
    half = (ffn_weight.shape[1]) // 3
    normed, inverse = norm(hidden, input_gain)
    proj = dot(normed, in_weight)
    mixed = mixer_forward(sizes, proj, side)
    middle = hidden + row_sum(dot(mixed, out_weight, NT).astype(bf16)).astype(f32)
    post, post_inverse = norm(middle, post_gain)
    wide = dot(post, ffn_weight[:, : 2 * half])
    gate, upper = wide[:, :half], wide[:, half:]
    active = (jax.nn.silu(gate) * upper).astype(bf16)
    output = middle + row_sum(dot(active, ffn_weight[:, 2 * half :], NT).astype(bf16)).astype(f32)
    return output, (hidden, inverse, normed, proj, mixed, middle, post_inverse, post, wide, active)


def layer_backward(grad, saved, params, sizes):
    input_gain, post_gain, in_weight, out_weight, ffn_weight, side = params
    hidden, inverse, normed, proj, mixed, middle, post_inverse, post, wide, active = saved
    half = (ffn_weight.shape[1]) // 3
    gate, upper = wide[:, :half], wide[:, half:]
    low = grad.astype(bf16)
    dactive = dot(low, ffn_weight[:, 2 * half :])
    lifted = jax.nn.sigmoid(gate)
    dgate = dactive * upper * lifted * (1.0 + gate * (1.0 - lifted))
    dwide = jnp.concatenate([dgate, dactive * gate * lifted], axis=1).astype(bf16)
    dpost = row_sum(dot(dwide, ffn_weight[:, : 2 * half], NT).astype(bf16)).astype(f32)
    ffn_grad = scatter_grad(
        jnp.concatenate([dot(post, dwide, TN), dot(low, active, TN)], axis=1)
    )
    dmiddle, post_gain_grad = norm_back(middle, post_inverse, post_gain, dpost)
    dmiddle = dmiddle + grad
    low = dmiddle.astype(bf16)
    dmix = dot(low, out_weight)
    out_grad = scatter_grad(dot(low, mixed, TN))
    dproj, dtaps, dheads = mixer_backward(sizes, proj, dmix, side)
    dnormed = row_sum(dot(dproj, in_weight, NT).astype(bf16)).astype(f32)
    in_grad = scatter_grad(dot(normed, dproj, TN))
    dhidden, input_gain_grad = norm_back(hidden, inverse, input_gain, dnormed)
    return dmiddle + dhidden, (
        ffn_grad,
        out_grad,
        in_grad,
        dtaps,
        dheads,
        input_gain_grad,
        post_gain_grad,
    )


def shards(
    hidden_in,
    segments,
    cotangent,
    input_gain,
    query_weight,
    keyval_weight,
    mixer_gate_weight,
    mixer_input_weight,
    state_weight,
    step_weight,
    conv_values,
    conv_shared,
    step_bias,
    decay_log,
    skip_gain,
    attention_out,
    mixer_out,
    post_gain,
    gate_weight,
    up_weight,
    down_weight,
):
    tokens = hidden_in.shape[0]
    row_index = lax.axis_index("row")
    col_index = lax.axis_index("col")
    query_cols = query_weight.shape[2]
    gate_cols = mixer_gate_weight.shape[2]
    input_cols = mixer_input_weight.shape[2]
    state_cols = state_weight.shape[2]
    heads_row = step_bias.shape[1]
    sizes = [0]
    for count in (query_cols, gate_cols, input_cols, state_cols, 2 * HEAD):
        sizes.append(sizes[-1] + count)
    sizes = tuple(sizes)
    kv_index = row_index * (query_cols // HEAD) // (HEADS // KV_HEADS)
    key_first = kv_index * HEAD
    value_first = KV_HEADS * HEAD + kv_index * HEAD
    step_first = row_index * heads_row

    in_local = jnp.concatenate(
        [
            query_weight,
            mixer_gate_weight,
            mixer_input_weight,
            state_weight,
            lax.dynamic_slice_in_dim(keyval_weight, key_first, HEAD, 2),
            lax.dynamic_slice_in_dim(keyval_weight, value_first, HEAD, 2),
            lax.dynamic_slice_in_dim(step_weight, step_first, heads_row, 2),
            jnp.zeros(step_weight.shape[:2] + (LANES - heads_row,), bf16),
        ],
        axis=2,
    )
    out_local = jnp.swapaxes(jnp.concatenate([attention_out, mixer_out], axis=1), 1, 2)
    ffn_local = jnp.concatenate([gate_weight, up_weight, jnp.swapaxes(down_weight, 1, 2)], axis=2)

    segment_ids = lax.dynamic_slice_in_dim(segments, col_index * tokens, tokens, 0)
    links = [jnp.ones((tokens,), f32)]
    for offset in range(1, 4):
        earlier = jnp.concatenate([jnp.full((offset,), -1, jnp.int32), segment_ids[:-offset]])
        links.append((earlier == segment_ids).astype(f32))
    links = jnp.pad(jnp.stack(links, axis=1), ((0, 8), (0, 4)))
    spread = (
        lax.broadcasted_iota(jnp.int32, (LANES, heads_row * M_HEAD), 0)
        == lax.broadcasted_iota(jnp.int32, (LANES, heads_row * M_HEAD), 1) // M_HEAD
    ).astype(f32)

    params = []
    for layer in range(LAYERS):
        heads = jnp.stack([step_bias[layer], jnp.exp(decay_log[layer])])
        side = (
            segment_ids[:, None],
            segment_ids[None, :],
            links,
            jnp.pad(
                jnp.concatenate([conv_values[layer], conv_shared[layer]], axis=1), ((0, 4), (0, 0))
            ),
            jnp.pad(heads, ((0, 6), (0, LANES - heads_row))),
            jnp.repeat(skip_gain[layer], M_HEAD)[None, :],
            spread,
        )
        params.append(
            (
                lax.all_gather(input_gain[layer], "col", axis=0, tiled=True),
                lax.all_gather(post_gain[layer], "col", axis=0, tiled=True),
                gather_weight(in_local[layer]),
                gather_weight(out_local[layer]),
                gather_weight(ffn_local[layer]),
                side,
            )
        )

    hidden = whole_features(hidden_in).astype(f32)
    grad = whole_features(cotangent).astype(f32)
    stored = []
    for layer in range(LAYERS):
        hidden, saved = layer_forward(hidden, params[layer], sizes)
        stored.append(saved)
    hidden_out = own_block(hidden.astype(bf16))
    collected = [None] * LAYERS
    for layer in reversed(range(LAYERS)):
        grad, collected[layer] = layer_backward(grad, stored[layer], params[layer], sizes)
    hidden_grad = own_block(grad)

    ffn_grad, out_grad, in_grad, dtaps, dheads, input_gain_grad, post_gain_grad = (
        jnp.stack([entry[member] for entry in collected]) for member in range(7)
    )
    first = sizes[3]
    states_part = in_grad[:, :, sizes[3] : sizes[4]].astype(f32)
    key_part = in_grad[:, :, sizes[4] : sizes[4] + HEAD].astype(f32)
    value_part = in_grad[:, :, sizes[4] + HEAD : sizes[5]].astype(f32)
    steps_part = in_grad[:, :, sizes[5] : sizes[5] + heads_row].astype(f32)
    keyval_part = jnp.zeros(keyval_weight.shape, f32)
    keyval_part = lax.dynamic_update_slice_in_dim(keyval_part, key_part, key_first, 2)
    keyval_part = lax.dynamic_update_slice_in_dim(keyval_part, value_part, value_first, 2)
    step_part = lax.dynamic_update_slice_in_dim(
        jnp.zeros(step_weight.shape, f32), steps_part, step_first, 2
    )
    shared_grad = lax.psum(
        jnp.concatenate([keyval_part, states_part, step_part], axis=2).astype(bf16), "row"
    ).astype(f32)
    kv_cols = keyval_weight.shape[2]
    dtaps, dheads, input_gain_grad, post_gain_grad = lax.psum(
        (dtaps, dheads, input_gain_grad, post_gain_grad), ("dp", "col")
    )
    conv_shared_grad = lax.psum(dtaps[:, :4, input_cols:], "row")
    features = hidden_in.shape[1]

    def own_gain(value):
        return lax.dynamic_slice_in_dim(value, col_index * features, features, 1)

    half = gate_weight.shape[2]
    attn_rows = attention_out.shape[1]
    out_grad = jnp.swapaxes(out_grad.astype(f32), 1, 2)
    return (
        hidden_out,
        hidden_grad,
        own_gain(input_gain_grad),
        in_grad[:, :, :query_cols].astype(f32),
        shared_grad[:, :, :kv_cols],
        in_grad[:, :, sizes[1] : sizes[2]].astype(f32),
        in_grad[:, :, sizes[2] : sizes[3]].astype(f32),
        shared_grad[:, :, kv_cols : kv_cols + state_cols],
        shared_grad[:, :, kv_cols + state_cols :],
        dtaps[:, :4, :input_cols],
        conv_shared_grad,
        dheads[:, 0, :heads_row],
        dheads[:, 1, :heads_row],
        dheads[:, 2, :heads_row],
        out_grad[:, :attn_rows, :],
        out_grad[:, attn_rows:, :],
        own_gain(post_gain_grad),
        ffn_grad[:, :, :half].astype(f32),
        ffn_grad[:, :, half : 2 * half].astype(f32),
        jnp.swapaxes(ffn_grad[:, :, 2 * half :].astype(f32), 1, 2),
    )


def solution(mesh):
    placed = (
        P(("dp", "row"), "col"),
        P("dp"),
        P(("dp", "row"), "col"),
        P(None, "col"),
        P(None, "col", "row"),
        P(None, "col", None),
        P(None, "col", "row"),
        P(None, "col", "row"),
        P(None, "col", None),
        P(None, "col", None),
        P(None, None, "row"),
        P(),
        P(None, "row"),
        P(None, "row"),
        P(None, "row"),
        P(None, "row", "col"),
        P(None, "row", "col"),
        P(None, "col"),
        P(None, "col", "row"),
        P(None, "col", "row"),
        P(None, "row", "col"),
    )
    return jax.shard_map(
        shards,
        mesh=mesh,
        in_specs=placed,
        out_specs=(
            P(("dp", "row"), "col"),
            P(("dp", "row"), "col"),
            P(None, "col"),
            P(None, "col", "row"),
            P(None, "col", None),
            P(None, "col", "row"),
            P(None, "col", "row"),
            P(None, "col", None),
            P(None, "col", None),
            P(None, None, "row"),
            P(),
            P(None, "row"),
            P(None, "row"),
            P(None, "row"),
            P(None, "row", "col"),
            P(None, "row", "col"),
            P(None, "col"),
            P(None, "col", "row"),
            P(None, "col", "row"),
            P(None, "row", "col"),
        ),
        check_vma=False,
    )
```

```python
from functools import partial

import jax
import jax.numpy as jnp
from jax import lax
from jax.experimental import pallas as pl
from jax.experimental.pallas import tpu as pltpu
from jax.sharding import PartitionSpec as P

HEADS = 8
KV_HEADS = 2
HEAD = 64
M_HEAD = 64
LAYERS = 2
LANES = 128
ROWS = 128

epsilon = 1e-05
highest = lax.Precision.HIGHEST
f32 = jnp.float32
bf16 = jnp.bfloat16

NN = (((1,), (0,)), ((), ()))
NT = (((1,), (1,)), ((), ()))
TN = (((0,), (0,)), ((), ()))


def dot(left, right, dims=NN, precision=None):
    return lax.dot_general(left, right, dims, precision=precision, preferred_element_type=f32)


def left_lanes():
    return lax.broadcasted_iota(jnp.int32, (ROWS, LANES), 1) < HEAD


def side_lanes():
    lane = lax.broadcasted_iota(jnp.int32, (ROWS, LANES), 1)
    return lane < HEAD, lane >= HEAD


def prepare(block, sizes, proj_ref, link_ref, taps_ref, heads_ref, spread_ref):
    first, last = block * ROWS, (block + 1) * ROWS
    conv_first, conv_last, steps_first = sizes[2], sizes[4], sizes[5]
    signal = proj_ref[first:last, conv_first:conv_last]
    if block == 0:
        prior = jnp.zeros((8, conv_last - conv_first), f32)
    else:
        prior = proj_ref[first - 8 : first, conv_first:conv_last]
    joined = jnp.concatenate([prior, signal], axis=0)
    pre = signal * taps_ref[0:1, :]
    for offset in range(1, 4):
        earlier = joined[8 - offset : 8 - offset + ROWS]
        pre = pre + earlier * taps_ref[offset : offset + 1, :] * link_ref[first:last, offset : offset + 1]
    raw = proj_ref[first:last, steps_first : steps_first + LANES] + heads_ref[0:1, :]
    steps = jnp.maximum(raw, 0.0) + jnp.log1p(jnp.exp(-jnp.abs(raw)))
    wide = dot(steps, spread_ref[...], NN, highest)
    return pre, raw, steps, wide


def running(steps, heads_ref, carry):
    lower = (
        lax.broadcasted_iota(jnp.int32, (ROWS, ROWS), 0)
        >= lax.broadcasted_iota(jnp.int32, (ROWS, ROWS), 1)
    ).astype(f32)
    return dot(lower, -steps * heads_ref[1:2, :], NN, highest) + carry


def key_value(block, sizes, proj_ref):
    pair = proj_ref[block * ROWS : (block + 1) * ROWS, sizes[4] : sizes[5]]
    turned = pltpu.roll(pair, HEAD, 1)
    left = left_lanes()
    return jnp.where(left, pair, turned).astype(bf16), jnp.where(left, turned, pair).astype(bf16)


def hidden_links(block, segc_ref, segr_ref):
    width = (block + 1) * ROWS
    token = lax.broadcasted_iota(jnp.int32, (ROWS, width), 0) + block * ROWS
    source = lax.broadcasted_iota(jnp.int32, (ROWS, width), 1)
    same = segc_ref[block * ROWS : width, :] == segr_ref[:, :width]
    return jnp.where((token >= source) & same, 0.0, -1e30)


def mixer_forward_kernel(
    sizes,
    proj_ref,
    segc_ref,
    segr_ref,
    link_ref,
    taps_ref,
    heads_ref,
    skip_ref,
    spread_ref,
    out_ref,
    inner_s,
    xdt_s,
    b_s,
    c_s,
    cum_s,
    turned_s,
    key_s,
    value_s,
):
    blocks = proj_ref.shape[0] // ROWS
    width = sizes[3] - sizes[2]
    carry = jnp.zeros((1, LANES), f32)
    for block in range(blocks):
        rows = slice(block * ROWS, (block + 1) * ROWS)
        pre, raw, steps, wide = prepare(
            block, sizes, proj_ref, link_ref, taps_ref, heads_ref, spread_ref
        )
        active = pre * jax.nn.sigmoid(pre)
        inner = active[:, :width]
        inner_s[rows, :] = inner
        xdt_s[rows, :] = (inner * wide).astype(bf16)
        b_s[rows, :] = active[:, width : width + LANES].astype(bf16)
        c_s[rows, :] = active[:, width + LANES :].astype(bf16)
        cum = running(steps, heads_ref, carry)
        carry = cum[ROWS - 1 :, :]
        cum_s[rows, :] = cum
        turned_s[:, rows] = cum.T
        key_s[rows, :], value_s[rows, :] = key_value(block, sizes, proj_ref)
    left = left_lanes()
    for block in range(blocks):
        rows = slice(block * ROWS, (block + 1) * ROWS)
        span = (block + 1) * ROWS
        bias = hidden_links(block, segc_ref, segr_ref)
        query = proj_ref[rows, : sizes[1]]
        parts = []
        for side in range(2):
            chosen = jnp.where(side_lanes()[side], query, 0.0).astype(bf16)
            scores = dot(chosen, key_s[:span, :], NT) * (HEAD**-0.5) + bias
            weights = jnp.exp(scores - jnp.max(scores, axis=1, keepdims=True))
            weights = weights * (1.0 / jnp.sum(weights, axis=1, keepdims=True))
            parts.append(dot(weights.astype(bf16), value_s[:span, :]))
        out_ref[rows, : sizes[1]] = jnp.where(left, parts[0], parts[1]).astype(bf16)
        affinity = dot(c_s[rows, :], b_s[:span, :], NT)
        for pair in range(width // LANES):
            cols = slice(pair * LANES, (pair + 1) * LANES)
            parts = []
            for side in range(2):
                head = 2 * pair + side
                decay = jnp.exp(
                    cum_s[rows, head : head + 1] - turned_s[head : head + 1, :span] + bias
                )
                parts.append(dot((affinity * decay).astype(bf16), xdt_s[:span, cols]))
            scanned = jnp.where(left, parts[0], parts[1])
            scanned = scanned + skip_ref[:, cols] * inner_s[rows, cols]
            gate = proj_ref[rows, sizes[1] + pair * LANES : sizes[1] + (pair + 1) * LANES]
            out_ref[rows, sizes[1] + pair * LANES : sizes[1] + (pair + 1) * LANES] = (
                scanned * gate * jax.nn.sigmoid(gate)
            ).astype(bf16)


def mixer_backward_kernel(
    sizes,
    proj_ref,
    dmix_ref,
    segc_ref,
    segr_ref,
    link_ref,
    taps_ref,
    heads_ref,
    skip_ref,
    spread_ref,
    dproj_ref,
    dtaps_ref,
    dheads_ref,
    inner_s,
    xdt_s,
    b_s,
    c_s,
    cum_s,
    turned_s,
    key_s,
    value_s,
    pre_s,
    dscan_s,
    dxdt_s,
    db_s,
    dc_s,
    dkey_s,
    dvalue_s,
    dcum_s,
    dpre_s,
):
    length = proj_ref.shape[0]
    blocks = length // ROWS
    width = sizes[3] - sizes[2]
    conv_first, conv_last, steps_first = sizes[2], sizes[4], sizes[5]
    conv_width = conv_last - conv_first
    carry = jnp.zeros((1, LANES), f32)
    for block in range(blocks):
        rows = slice(block * ROWS, (block + 1) * ROWS)
        pre, raw, steps, wide = prepare(
            block, sizes, proj_ref, link_ref, taps_ref, heads_ref, spread_ref
        )
        pre_s[rows, :] = pre
        active = pre * jax.nn.sigmoid(pre)
        inner = active[:, :width]
        inner_s[rows, :] = inner
        xdt_s[rows, :] = (inner * wide).astype(bf16)
        b_s[rows, :] = active[:, width : width + LANES].astype(bf16)
        c_s[rows, :] = active[:, width + LANES :].astype(bf16)
        cum = running(steps, heads_ref, carry)
        carry = cum[ROWS - 1 :, :]
        cum_s[rows, :] = cum
        turned_s[:, rows] = cum.T
        key_s[rows, :], value_s[rows, :] = key_value(block, sizes, proj_ref)
    dxdt_s[...] = jnp.zeros_like(dxdt_s)
    db_s[...] = jnp.zeros_like(db_s)
    dkey_s[...] = jnp.zeros_like(dkey_s)
    dvalue_s[...] = jnp.zeros_like(dvalue_s)
    left = left_lanes()
    dskip = jnp.zeros((1, width), f32)
    for block in range(blocks):
        rows = slice(block * ROWS, (block + 1) * ROWS)
        span = (block + 1) * ROWS
        bias = hidden_links(block, segc_ref, segr_ref)
        query = proj_ref[rows, : sizes[1]]
        dattended = dmix_ref[rows, : sizes[1]]
        parts = []
        for side in range(2):
            own = side_lanes()[side]
            chosen = jnp.where(own, query, 0.0).astype(bf16)
            dchosen = jnp.where(own, dattended, 0.0).astype(bf16)
            scores = dot(chosen, key_s[:span, :], NT) * (HEAD**-0.5) + bias
            weights = jnp.exp(scores - jnp.max(scores, axis=1, keepdims=True))
            weights = weights * (1.0 / jnp.sum(weights, axis=1, keepdims=True))
            dweights = dot(dchosen, value_s[:span, :], NT)
            dvalue_s[:span, :] += dot(weights.astype(bf16), dchosen, TN)
            mean = jnp.sum(weights * dweights, axis=1, keepdims=True)
            dscores = (weights * (dweights - mean) * (HEAD**-0.5)).astype(bf16)
            parts.append(dot(dscores, key_s[:span, :]))
            dkey_s[:span, :] += dot(dscores, chosen, TN)
        dproj_ref[rows, : sizes[1]] = jnp.where(left, parts[0], parts[1]).astype(bf16)
        affinity = dot(c_s[rows, :], b_s[:span, :], NT)
        daffinity = jnp.zeros((ROWS, span), f32)
        dcum = jnp.zeros((ROWS, LANES), f32)
        for pair in range(width // LANES):
            cols = slice(pair * LANES, (pair + 1) * LANES)
            gate_cols = slice(sizes[1] + pair * LANES, sizes[1] + (pair + 1) * LANES)
            gate = proj_ref[rows, gate_cols]
            lifted = jax.nn.sigmoid(gate)
            dmamba = dmix_ref[rows, gate_cols]
            dscan = dmamba * gate * lifted
            dscan_s[rows, cols] = dscan
            parts, mixes, sides = [], [], []
            for side in range(2):
                head = 2 * pair + side
                decay = jnp.exp(
                    cum_s[rows, head : head + 1] - turned_s[head : head + 1, :span] + bias
                )
                mix = (affinity * decay).astype(bf16)
                dside = jnp.where(side_lanes()[side], dscan, 0.0).astype(bf16)
                daffinity = daffinity + dot(dside, xdt_s[:span, cols], NT) * decay
                parts.append(dot(mix, xdt_s[:span, cols]))
                mixes.append(mix)
                sides.append(dside)
            dxdt_s[:span, cols] += dot(
                jnp.concatenate(mixes, axis=0), jnp.concatenate(sides, axis=0), TN
            )
            scanned = jnp.where(left, parts[0], parts[1])
            inner = inner_s[rows, cols]
            dcum = dcum + dot(
                scanned * dscan.astype(bf16).astype(f32), spread_ref[:, cols], NT, highest
            )
            scanned = scanned + skip_ref[:, cols] * inner
            dproj_ref[rows, gate_cols] = (
                dmamba * scanned * lifted * (1.0 + gate * (1.0 - lifted))
            ).astype(bf16)
        dcum_s[rows, :] = dcum
        dskip = dskip + jnp.sum(dscan_s[rows, :] * inner_s[rows, :], axis=0, keepdims=True)
        daffinity = daffinity.astype(bf16)
        dc_s[rows, :] = dot(daffinity, b_s[:span, :])
        db_s[:span, :] += dot(daffinity, c_s[rows, :], TN)
    upper = (
        lax.broadcasted_iota(jnp.int32, (ROWS, ROWS), 0)
        <= lax.broadcasted_iota(jnp.int32, (ROWS, ROWS), 1)
    ).astype(f32)
    carry = jnp.zeros((1, LANES), f32)
    dbias = jnp.zeros((1, LANES), f32)
    drate = jnp.zeros((1, LANES), f32)
    dpre_s[length:, :] = jnp.zeros((8, conv_width), f32)
    for block in reversed(range(blocks)):
        rows = slice(block * ROWS, (block + 1) * ROWS)
        raw = proj_ref[rows, steps_first : steps_first + LANES] + heads_ref[0:1, :]
        steps = jnp.maximum(raw, 0.0) + jnp.log1p(jnp.exp(-jnp.abs(raw)))
        wide = dot(steps, spread_ref[...], NN, highest)
        dxdt = dxdt_s[rows, :]
        dcum = dcum_s[rows, :] - dot(
            xdt_s[rows, :].astype(f32) * dxdt, spread_ref[...], NT, highest
        )
        dlog = dot(upper, dcum, NN, highest) + carry
        carry = dlog[0:1, :]
        dsteps = (
            dot(dxdt * inner_s[rows, :], spread_ref[...], NT, highest) - heads_ref[1:2, :] * dlog
        )
        drate = drate - jnp.sum(steps * dlog, axis=0, keepdims=True)
        draw = dsteps * jax.nn.sigmoid(raw)
        dbias = dbias + jnp.sum(draw, axis=0, keepdims=True)
        dproj_ref[rows, steps_first : steps_first + LANES] = draw.astype(bf16)
        dinner = dxdt * wide + skip_ref[...] * dscan_s[rows, :]
        dactive = jnp.concatenate([dinner, db_s[rows, :], dc_s[rows, :]], axis=1)
        pre = pre_s[rows, :]
        lifted = jax.nn.sigmoid(pre)
        dpre_s[rows, :] = dactive * lifted * (1.0 + pre * (1.0 - lifted))
        dkey = dkey_s[rows, :]
        dvalue = dvalue_s[rows, :]
        dkey = dkey + pltpu.roll(dkey, HEAD, 1)
        dvalue = dvalue + pltpu.roll(dvalue, HEAD, 1)
        dproj_ref[rows, conv_last:steps_first] = jnp.where(left, dkey, dvalue).astype(bf16)
    dtaps = [jnp.zeros((1, conv_width), f32) for _ in range(4)]
    for block in range(blocks):
        first, last = block * ROWS, (block + 1) * ROWS
        signal = proj_ref[first:last, conv_first:conv_last]
        joined = dpre_s[first : last + 8, :]
        own = joined[:ROWS]
        dsignal = own * taps_ref[0:1, :]
        dtaps[0] = dtaps[0] + jnp.sum(signal * own, axis=0, keepdims=True)
        for offset in range(1, 4):
            later = (joined * link_ref[first : last + 8, offset : offset + 1])[
                offset : offset + ROWS
            ]
            dsignal = dsignal + later * taps_ref[offset : offset + 1, :]
            dtaps[offset] = dtaps[offset] + jnp.sum(signal * later, axis=0, keepdims=True)
        dproj_ref[first:last, conv_first:conv_last] = dsignal.astype(bf16)
    dtaps_ref[...] = jnp.concatenate(dtaps + [jnp.zeros((4, conv_width), f32)], axis=0)
    dheads_ref[...] = jnp.concatenate(
        [
            dbias,
            drate * heads_ref[1:2, :],
            dot(dskip, spread_ref[...], NT, highest),
            jnp.zeros((5, LANES), f32),
        ],
        axis=0,
    )


def shared_scratch(length, width):
    return [
        pltpu.VMEM((length, width), f32),
        pltpu.VMEM((length, width), bf16),
        pltpu.VMEM((length, LANES), bf16),
        pltpu.VMEM((length, LANES), bf16),
        pltpu.VMEM((length, LANES), f32),
        pltpu.VMEM((LANES, length), f32),
        pltpu.VMEM((length, LANES), bf16),
        pltpu.VMEM((length, LANES), bf16),
    ]


def fetch(plan, refs, target, semaphores):
    col = lax.axis_index("col")
    whole = target.shape[0] // 2
    copies = []
    for index, (piece, first, rows, half, distance, source, place, count) in enumerate(plan):
        if isinstance(half, tuple):
            at = pl.multiple_of((half[0] ^ (lax.axis_index("dp") & 1)) * whole, rows)
        else:
            at = half * whole
        if isinstance(distance, tuple):
            at = pl.multiple_of(at + distance[0] * rows, rows)
        elif distance is not None:
            at = pl.multiple_of(at + (col ^ distance) * rows, rows)
        copy = pltpu.make_async_copy(
            refs[piece].at[pl.ds(first, rows), pl.ds(source, count)],
            target.at[pl.ds(at, rows), pl.ds(place, count)],
            semaphores.at[index],
        )
        copy.start()
        copies.append(copy)
    return copies


def arrived(copies):
    for copy in copies:
        copy.wait()


def own_rows(length):
    half = length // 2
    parity = lax.axis_index("row") & 1
    return (
        pl.ds(pl.multiple_of(parity * half, half), half),
        pl.ds(pl.multiple_of((1 - parity) * half, half), half),
    )


def by_rows(length, body):
    def step(index, carry):
        body(pl.ds(pl.multiple_of(index * ROWS, ROWS), ROWS))
        return carry

    lax.fori_loop(0, length // ROWS, step, 0)


def add_sum(base_ref, sum_refs, total_ref):
    for rows, part in zip(own_rows(base_ref.shape[0]), sum_refs):
        total_ref[rows, :] = base_ref[rows, :] + part[...].astype(f32)


def norm_rows(hidden_ref, gain_ref, normed_ref):
    def body(rows):
        hidden = hidden_ref[rows, :]
        inverse = lax.rsqrt(jnp.mean(hidden * hidden, axis=1, keepdims=True) + epsilon)
        normed_ref[rows, :] = (hidden * inverse * gain_ref[...]).astype(bf16)

    by_rows(hidden_ref.shape[0], body)


def norm_back_rows(hidden_ref, gain_ref, grad_ref, base_ref, total_ref, low_ref, dgain_ref):
    dgain_ref[...] = jnp.zeros_like(dgain_ref)

    def body(rows):
        hidden, grad = hidden_ref[rows, :], grad_ref[rows, :].astype(f32)
        inverse = lax.rsqrt(jnp.mean(hidden * hidden, axis=1, keepdims=True) + epsilon)
        weighted = grad * gain_ref[...]
        mean = jnp.mean(weighted * hidden, axis=1, keepdims=True)
        total = base_ref[rows, :] + (
            inverse * weighted - hidden * (inverse * inverse * inverse * mean)
        )
        total_ref[rows, :] = total
        low_ref[rows, :] = total.astype(bf16)
        dgain_ref[...] += jnp.sum(grad * hidden * inverse, axis=0, keepdims=True)

    by_rows(hidden_ref.shape[0], body)


def set_sum(sum_refs, total_ref):
    for rows, part in zip(own_rows(total_ref.shape[0]), sum_refs):
        total_ref[rows, :] = part[...]


def times(left_ref, weight_ref, first, last, result_ref, place=0, dims=NN):
    for column in range(first, last, 256):
        count = min(256, last - column)
        result_ref[:, place + column - first : place + column - first + count] = dot(
            left_ref[...], weight_ref[:, column : column + count]
        ).astype(result_ref.dtype)


def parts(left_ref, weight_ref, first, last, kept_ref, away_ref):
    for rows, part_ref in zip(own_rows(left_ref.shape[0]), (kept_ref, away_ref)):
        left = left_ref[rows, :]
        for feature in range(0, weight_ref.shape[0], 256):
            part_ref[:, feature : feature + 256] = dot(
                left, weight_ref[feature : feature + 256, first:last], NT
            ).astype(bf16)


def take(refs, *counts):
    taken = []
    for count in counts:
        taken.append(refs[:count])
        refs = refs[count:]
    return taken


def first_kernel(sizes, plans, counts, *refs):
    ins, outs, scratch = take(refs, *counts[:3])
    summed = len(ins) - counts[3] - 9 == 2
    base_ref, gain_ref = ins[:2]
    side = ins[2:9]
    sums, pieces = ins[9 : len(ins) - counts[3]], ins[len(ins) - counts[3] :]
    hidden_ref, normed_ref, proj_ref, mixed_ref, kept_ref, away_ref = outs
    in_ref, out_ref, in_sems, out_sems = scratch[:4]
    waits = fetch(plans[0], pieces, in_ref, in_sems)
    out_waits = fetch(plans[1], pieces, out_ref, out_sems)
    if summed:
        add_sum(base_ref, sums, hidden_ref)
    else:
        hidden_ref[...] = base_ref[...].astype(f32)
    norm_rows(hidden_ref, gain_ref, normed_ref)
    arrived(waits)
    times(normed_ref, in_ref, 0, in_ref.shape[1], proj_ref)
    mixer_forward_kernel(sizes, proj_ref, *side, mixed_ref, *scratch[4:])
    arrived(out_waits)
    parts(mixed_ref, out_ref, 0, out_ref.shape[1], kept_ref, away_ref)


def second_kernel(plans, counts, *refs):
    ins, outs, scratch = take(refs, *counts[:3])
    hidden_ref, gain_ref, kept_sum, other_sum = ins[:4]
    middle_ref, post_ref, wide_ref, active_ref, kept_ref, away_ref = outs
    ffn_ref, sems = scratch
    waits = fetch(plans[0], ins[4:], ffn_ref, sems)
    add_sum(hidden_ref, (kept_sum, other_sum), middle_ref)
    norm_rows(middle_ref, gain_ref, post_ref)
    arrived(waits)
    half = ffn_ref.shape[1] // 3
    times(post_ref, ffn_ref, 0, 2 * half, wide_ref)

    def body(rows):
        gate, upper = wide_ref[rows, :half], wide_ref[rows, half:]
        active_ref[rows, :] = (gate * jax.nn.sigmoid(gate) * upper).astype(bf16)

    by_rows(wide_ref.shape[0], body)
    parts(active_ref, ffn_ref, 2 * half, 3 * half, kept_ref, away_ref)


def third_kernel(plans, counts, *refs):
    ins, outs, scratch = take(refs, *counts[:3])
    ffn_ref, sems, dactive_ref = scratch[:3]
    wide_ref = ins[0]
    pieces = ins[len(ins) - counts[3] :]
    waits = fetch(plans[0], pieces, ffn_ref, sems)
    low_ref, dwide_ref, kept_ref, away_ref = outs[:4]
    if len(outs) == 6:
        hidden_ref, gain_ref, base_ref, kept_sum, other_sum = ins[1:6]
        grad_ref, dgain_ref = outs[4:]
        dnormed_ref = scratch[3]
        set_sum((kept_sum, other_sum), dnormed_ref)
        norm_back_rows(hidden_ref, gain_ref, dnormed_ref, base_ref, grad_ref, low_ref, dgain_ref)
    else:
        low_ref[...] = ins[1][...].astype(bf16)
    arrived(waits)
    half = ffn_ref.shape[1] // 3
    times(low_ref, ffn_ref, 2 * half, 3 * half, dactive_ref)

    def body(rows):
        gate, upper = wide_ref[rows, :half], wide_ref[rows, half:]
        dactive = dactive_ref[rows, :]
        lifted = jax.nn.sigmoid(gate)
        dwide_ref[rows, :half] = (
            dactive * upper * lifted * (1.0 + gate * (1.0 - lifted))
        ).astype(bf16)
        dwide_ref[rows, half:] = (dactive * gate * lifted).astype(bf16)

    by_rows(wide_ref.shape[0], body)
    parts(dwide_ref, ffn_ref, 0, 2 * half, kept_ref, away_ref)


def fourth_kernel(sizes, plans, counts, *refs):
    ins, outs, scratch = take(refs, *counts[:3])
    base_ref, middle_ref, gain_ref, kept_sum, other_sum, proj_ref = ins[:6]
    side = ins[6:13]
    pieces = ins[len(ins) - counts[3] :]
    dmiddle_ref, low_ref, dgain_ref, dproj_ref, dtaps_ref, dheads_ref, kept_ref, away_ref = outs
    in_ref, out_ref, in_sems, out_sems, dpost_ref, dmix_ref = scratch[:6]
    out_waits = fetch(plans[1], pieces, out_ref, out_sems)
    waits = fetch(plans[0], pieces, in_ref, in_sems)
    set_sum((kept_sum, other_sum), dpost_ref)
    norm_back_rows(middle_ref, gain_ref, dpost_ref, base_ref, dmiddle_ref, low_ref, dgain_ref)
    arrived(out_waits)
    times(low_ref, out_ref, 0, out_ref.shape[1], dmix_ref)
    mixer_backward_kernel(
        sizes, proj_ref, dmix_ref, *side, dproj_ref, dtaps_ref, dheads_ref, *scratch[6:]
    )
    arrived(waits)
    parts(dproj_ref, in_ref, 0, in_ref.shape[1], kept_ref, away_ref)


def run_kernel(kernel, name, ins, pieces, out_shapes, scratch, waited=(), flops=10**9):
    vmem, anywhere = pl.BlockSpec(memory_space=pltpu.VMEM), pl.BlockSpec(memory_space=pl.ANY)
    arrays = list(ins) + list(waited) + list(pieces)
    counts = (len(arrays), len(out_shapes), len(scratch), len(pieces) + len(waited))

    def body(*refs):
        ordered = list(refs)
        first = len(ins)
        ordered[first : first + len(waited) + len(pieces)] = (
            refs[first + len(waited) : len(arrays)] + refs[first : first + len(waited)]
        )
        kernel(counts, *ordered)

    return pl.pallas_call(
        body,
        out_shape=out_shapes,
        in_specs=[vmem] * len(ins) + [anywhere] * (len(waited) + len(pieces)),
        out_specs=[vmem] * len(out_shapes),
        scratch_shapes=scratch,
        compiler_params=pltpu.CompilerParams(vmem_limit_bytes=56 * 1024 * 1024),
        cost_estimate=pl.CostEstimate(
            flops=flops, bytes_accessed=10**7, transcendentals=10**6
        ),
        name=name,
    )(*arrays)


def shape(kind, *sizes):
    return jax.ShapeDtypeStruct(sizes, kind)


def swap(value, axis, distance):
    size = lax.axis_size(axis)
    return lax.ppermute(value, axis, [(i, i ^ distance) for i in range(size)])


def after(value, other):
    last = tuple(size - 1 for size in other.shape)
    ready = jnp.logical_not(other[last].astype(f32) > 3.3e38)
    return jnp.where(ready, value, jnp.zeros_like(value))


def bound(value, *others):
    for other in others:
        value = after(value, other)
    return value


def add(left, right):
    return (left.astype(f32) + right.astype(f32)).astype(bf16)


def row_steps(kept, away):
    middle = add(kept, swap(away, "row", 1))
    kept = add(middle, swap(middle, "row", 2))
    return middle, (kept, swap(kept, "row", 1))


def row_sum(kept, away):
    return row_steps(kept, away)[1]


def in_order(own, other, own_is_second, axis):
    return jnp.where(
        own_is_second == 0,
        jnp.concatenate([own, other], axis=axis),
        jnp.concatenate([other, own], axis=axis),
    )


def half_index():
    return lax.axis_index("dp") & 1


def turn(value, axis):
    low, high = jnp.split(value, 2, axis=axis)
    return in_order(low, high, half_index(), axis)


def by_half(value):
    pieces = jnp.split(value, value.shape[1] // LANES, axis=1)
    return jnp.concatenate(pieces[0::2] + pieces[1::2], axis=1)


def by_block(value):
    count = value.shape[1] // LANES // 2
    pieces = jnp.split(value, 2 * count, axis=1)
    return jnp.concatenate(
        [pieces[half * count + block] for block in range(count) for half in range(2)], axis=1
    )


def transpose_blocks(value):
    rows, cols = lax.axis_size("row"), lax.axis_size("col")
    pairs = [(r * cols + c, c * cols + r) for r in range(rows) for c in range(cols)]
    return lax.ppermute(value, ("row", "col"), pairs)


def whole_features(value):
    block = transpose_blocks(turn(value, 1))
    row = lax.axis_index("row")
    pair = in_order(block, swap(block, "row", 1), row & 1, 1)
    return by_half(in_order(pair, swap(pair, "row", 2), row >> 1, 1))


def own_features(value):
    row = lax.axis_index("row")
    halves = [
        lax.dynamic_slice_in_dim(piece, row * LANES, LANES, 1)
        for piece in jnp.split(value, 2, axis=1)
    ]
    return transpose_blocks(turn(jnp.concatenate(halves, axis=1), 1))


def gather_first(chunks):
    halves = [jnp.split(turn(chunk, 0), 2, axis=0) for chunk in chunks]
    gathered, seconds, earlier = [], [], None
    for mine, _ in halves:
        if earlier is not None:
            mine = after(mine, earlier)
        seconds.append(swap(mine, "col", 2))
        earlier = seconds[-1]
    for (mine, theirs), second in zip(halves, seconds):
        pair = swap(jnp.concatenate([mine, second], axis=0), "col", 1)
        others = swap(jnp.concatenate([second, pair], axis=0), "dp", 1)
        gathered.append((mine, second, pair, theirs, others))
    return gathered


def first_plan(base, rows, columns):
    places = [(0, 0, 0, 0), (2, 0, 0, 1), (1, 0, 0, 2), (2, rows, 0, 3)]
    places += [(3, 0, 1, 0), (4, rows, 1, 1), (4, 0, 1, 2), (4, 2 * rows, 1, 3)]
    return [(base + piece, first, rows, half, distance, *columns) for piece, first, half, distance in places]


def gather_later(weight, earlier):
    half = weight.shape[0] // 2
    mine, theirs = jnp.split(turn(weight, 0), 2, axis=0)
    whole = lax.all_gather(after(mine, earlier), "col", axis=0, tiled=True)
    col = lax.axis_index("col")
    others = [lax.dynamic_slice_in_dim(whole, (col ^ k) * half, half, 0) for k in range(1, 4)]
    return (whole, theirs, swap(jnp.concatenate(others, axis=0), "dp", 1))


def later_plan(rows, blocks, columns):
    places = [(0, 0, rows * blocks, 0, None), (1, 0, rows, 1, 0)]
    places += [(2, (k - 1) * rows, rows, 1, k) for k in range(1, 4)]
    return [(*place, *columns) for place in places]


def gather_whole(weight, earlier):
    return (lax.all_gather(after(weight, earlier), "col", axis=0, tiled=True),)


def whole_plan(rows, blocks, columns):
    return [
        (0, (2 * block + half) * rows, rows, (half,), (block,), *columns)
        for block in range(blocks)
        for half in range(2)
    ]


def three_parts(value):
    high = lax.reduce_precision(value, 8, 7)
    rest = value - high
    middle = lax.reduce_precision(rest, 8, 7)
    return [high.astype(bf16), middle.astype(bf16), (rest - middle).astype(bf16)]


def other_batches(value):
    size = lax.axis_size("dp")
    if size == 2:
        return value
    groups = [list(range(0, size, 2)), list(range(1, size, 2))]
    return lax.psum(value, "dp", axis_index_groups=groups)


def col_scatter(value):
    return other_batches(lax.psum_scatter(value, "col", scatter_dimension=0, tiled=True))


def add_kernel(counts, *refs):
    ins, outs, _ = take(refs, *counts[:3])

    def body(rows):
        outs[0][rows, :] = (ins[0][rows, :].astype(f32) + ins[1][rows, :].astype(f32)).astype(bf16)

    by_rows(outs[0].shape[0], body)


def dp_sum(mine, received, *waited):
    outs = (jax.ShapeDtypeStruct(mine.shape, bf16),)
    return run_kernel(add_kernel, "sum_halves", (mine, received), (), outs, [], waited)[0]


def sum_batches(value):
    return add(value, swap(value, "dp", 1))


def other_half(value):
    return in_order(value, swap(value, "dp", 1), half_index(), 0)


def sum_small(value):
    value = value + swap(value, "col", 1)
    value = value + swap(value, "col", 2)
    if lax.axis_size("dp") != 2:
        return lax.psum(value, "dp")
    return value + swap(value, "dp", 1)


def sum_row_small(value):
    value = value + swap(value, "row", 1)
    return value + swap(value, "row", 2)


def in_blocks(value):
    value = value.reshape(2, -1, LANES)
    value = jnp.where(half_index() == 0, value, value[::-1])
    return jnp.swapaxes(value, 0, 1).reshape(-1)


def mixer_scratch(plan, out_plan, features, in_cols, out_cols):
    return [
        pltpu.VMEM((features, in_cols), bf16),
        pltpu.VMEM((features, out_cols), bf16),
        pltpu.SemaphoreType.DMA((len(plan),)),
        pltpu.SemaphoreType.DMA((len(out_plan),)),
    ]


def layer_forward(base, sums, params, sizes, waited):
    input_gain, post_gain, mixer_pieces, plans, ffn_pieces, ffn_plan, side, in_cols, ffn_cols = params
    length, features = base.shape
    out_cols, width = sizes[2], sizes[3] - sizes[2]
    part = shape(bf16, length // 2, features)
    hidden, normed, proj, mixed, kept, away = run_kernel(
        partial(first_kernel, sizes, plans),
        "norm_mixer_out",
        (base, input_gain, *side, *sums),
        mixer_pieces,
        (
            shape(f32, length, features),
            shape(bf16, length, features),
            shape(f32, length, in_cols),
            shape(bf16, length, out_cols),
            part,
            part,
        ),
        mixer_scratch(*plans, features, in_cols, out_cols) + shared_scratch(length, width),
        waited,
        flops=10**7,
    )
    middle, post, wide, active, kept, away = run_kernel(
        partial(second_kernel, (ffn_plan,)),
        "norm_feed_forward",
        (hidden, post_gain, *row_sum(kept, away)),
        ffn_pieces,
        (
            shape(f32, length, features),
            shape(bf16, length, features),
            shape(f32, length, 2 * ffn_cols),
            shape(bf16, length, ffn_cols),
            part,
            part,
        ),
        [
            pltpu.VMEM((features, 3 * ffn_cols), bf16),
            pltpu.SemaphoreType.DMA((len(ffn_plan),)),
        ],
        flops=2 * 10**9,
    )
    return middle, row_sum(kept, away), (hidden, normed, proj, mixed, middle, post, wide, active)


def layer_backward(grad, above, saved, params, sizes, layer, waited):
    input_gain, post_gain, mixer_pieces, plans, ffn_pieces, ffn_plan, side, in_cols, ffn_cols = params
    hidden, normed, proj, mixed, middle, post, wide, active = saved
    length, features = hidden.shape
    own = features // 2
    out_cols, width, conv_width = sizes[2], sizes[3] - sizes[2], sizes[4] - sizes[2]
    part = shape(bf16, length // 2, features)
    outs = [shape(bf16, length, features), shape(bf16, length, 2 * ffn_cols), part, part]
    scratch = [
        pltpu.VMEM((features, 3 * ffn_cols), bf16),
        pltpu.SemaphoreType.DMA((len(ffn_plan),)),
        pltpu.VMEM((length, ffn_cols), f32),
    ]
    if above is None:
        ins = (wide, grad)
    else:
        ins = (wide, *above)
        outs += [shape(f32, length, features), shape(f32, 1, features)]
        scratch.append(pltpu.VMEM((length, features), bf16))
    low, dwide, kept, away, *rest = run_kernel(
        partial(third_kernel, (ffn_plan,)),
        "feed_forward_back",
        ins,
        ffn_pieces,
        tuple(outs),
        scratch,
        waited[0],
        flops=2 * 10**9,
    )
    gain_above = None
    if above is not None:
        grad, gain_above = rest
    total = row_sum(kept, away)
    last = layer == LAYERS - 1
    theirs = jnp.concatenate(
        [
            dot(post[:, own:], dwide, TN).astype(bf16),
            dot(low[:, own:], active, TN).astype(bf16),
        ],
        axis=1,
    )
    mine = jnp.concatenate(
        [
            dot(post[:, :own], dwide, TN).astype(bf16),
            dot(low[:, :own], active, TN).astype(bf16),
        ],
        axis=1,
    )
    wide_mine, wide_received, wide_tie = mine, swap(theirs, "dp", 1), total[1]
    before = (mine, theirs) + tuple(waited[1])
    if not last:
        later = add(waited[2][0], after(waited[2][1], total[1]))
        later_sum = col_scatter(later)
        before += (later,)
    dmiddle, low, post_gain_grad, dproj, dtaps, dheads, kept, away = run_kernel(
        partial(fourth_kernel, sizes, plans),
        "norm_mixer_back",
        (grad, middle, post_gain, *total, proj, *side),
        mixer_pieces,
        (
            shape(f32, length, features),
            shape(bf16, length, features),
            shape(f32, 1, features),
            shape(bf16, length, in_cols),
            shape(f32, 8, conv_width),
            shape(f32, 8, LANES),
            part,
            part,
        ),
        mixer_scratch(*plans, features, in_cols, out_cols)
        + [pltpu.VMEM((length, features), bf16), pltpu.VMEM((length, out_cols), f32)]
        + shared_scratch(length, width)
        + [
            pltpu.VMEM((length, conv_width), f32),
            pltpu.VMEM((length, width), f32),
            pltpu.VMEM((length, width), f32),
            pltpu.VMEM((length, LANES), f32),
            pltpu.VMEM((length, LANES), f32),
            pltpu.VMEM((length, LANES), f32),
            pltpu.VMEM((length, LANES), f32),
            pltpu.VMEM((length, LANES), f32),
            pltpu.VMEM((length + 8, conv_width), f32),
        ],
        before,
        flops=5 * 10**9,
    )
    total = row_sum(kept, away)
    if last:
        wide = add(wide_mine, after(wide_received, wide_tie))
        theirs_out = dot(low[:, own:], mixed, TN).astype(bf16)
        out_received = swap(theirs_out, "dp", 1)
        mine_out = dot(low[:, :own], mixed, TN).astype(bf16)
        out = add(mine_out, after(out_received, total[0]))
        theirs = dot(normed[:, own:], dproj, TN).astype(bf16)
        mine = dot(normed[:, :own], dproj, TN).astype(bf16)
        in_received = swap(theirs, "dp", 1)
        wide_sum, out_sum = col_scatter(wide), col_scatter(out)
        waited = ((theirs, mine, wide, out), (wide_sum,), (mine, in_received))
        sums = (wide_sum, out_sum)
    else:
        theirs = jnp.concatenate(
            [
                dot(normed[:, own:], dproj, TN).astype(bf16),
                dot(low[:, own:], mixed, TN).astype(bf16),
            ],
            axis=1,
        )
        received = swap(theirs, "dp", 1)
        mine = jnp.concatenate(
            [
                dot(normed[:, :own], dproj, TN).astype(bf16),
                dot(low[:, :own], mixed, TN).astype(bf16),
            ],
            axis=1,
        )
        whole = dp_sum(mine, received, total[0], later_sum)
        wide = dp_sum(wide_mine, wide_received, whole)
        sums = (col_scatter(wide), col_scatter(whole), later_sum, wide)
    above = (hidden, input_gain, dmiddle, *total)
    return above, waited, gain_above, post_gain_grad, dheads, dtaps, sums


def last_norm_back(hidden, gain, base, kept, other):
    grad = in_order(kept, other, lax.axis_index("row") & 1, 0).astype(f32)
    inverse = lax.rsqrt(jnp.mean(hidden * hidden, axis=1, keepdims=True) + epsilon)
    weighted = grad * gain
    mean = jnp.mean(weighted * hidden, axis=1, keepdims=True)
    total = base + inverse * weighted - hidden * (inverse * inverse * inverse * mean)
    return total, jnp.sum(grad * hidden * inverse, axis=0)


def shards(
    hidden_in,
    segments,
    cotangent,
    input_gain,
    query_weight,
    keyval_weight,
    mixer_gate_weight,
    mixer_input_weight,
    state_weight,
    step_weight,
    conv_values,
    conv_shared,
    step_bias,
    decay_log,
    skip_gain,
    attention_out,
    mixer_out,
    post_gain,
    gate_weight,
    up_weight,
    down_weight,
):
    tokens = hidden_in.shape[0]
    row_index = lax.axis_index("row")
    col_index = lax.axis_index("col")
    query_cols = query_weight.shape[2]
    gate_cols = mixer_gate_weight.shape[2]
    input_cols = mixer_input_weight.shape[2]
    state_cols = state_weight.shape[2]
    heads_row = step_bias.shape[1]
    sizes = [0]
    for count in (query_cols, gate_cols, input_cols, state_cols, 2 * HEAD):
        sizes.append(sizes[-1] + count)
    sizes = tuple(sizes)
    kv_index = row_index * (query_cols // HEAD) // (HEADS // KV_HEADS)
    key_first = kv_index * HEAD
    value_first = KV_HEADS * HEAD + kv_index * HEAD
    step_first = row_index * heads_row

    in_local = jnp.concatenate(
        [
            query_weight,
            mixer_gate_weight,
            mixer_input_weight,
            state_weight,
            lax.dynamic_slice_in_dim(keyval_weight, key_first, HEAD, 2),
            lax.dynamic_slice_in_dim(keyval_weight, value_first, HEAD, 2),
            lax.dynamic_slice_in_dim(step_weight, step_first, heads_row, 2),
            jnp.zeros(step_weight.shape[:2] + (LANES - heads_row,), bf16),
        ],
        axis=2,
    )
    out_local = jnp.swapaxes(jnp.concatenate([attention_out, mixer_out], axis=1), 1, 2)
    ffn_local = jnp.concatenate([gate_weight, up_weight, jnp.swapaxes(down_weight, 1, 2)], axis=2)

    segment_ids = lax.dynamic_slice_in_dim(segments, col_index * tokens, tokens, 0)
    links = [jnp.ones((tokens,), f32)]
    for offset in range(1, 4):
        earlier = jnp.concatenate([jnp.full((offset,), -1, jnp.int32), segment_ids[:-offset]])
        links.append((earlier == segment_ids).astype(f32))
    links = jnp.pad(jnp.stack(links, axis=1), ((0, 8), (0, 4)))
    spread = (
        lax.broadcasted_iota(jnp.int32, (LANES, heads_row * M_HEAD), 0)
        == lax.broadcasted_iota(jnp.int32, (LANES, heads_row * M_HEAD), 1) // M_HEAD
    ).astype(f32)

    sides = []
    for layer in range(LAYERS):
        heads = jnp.stack([step_bias[layer], jnp.exp(decay_log[layer])])
        side = (
            segment_ids[:, None],
            segment_ids[None, :],
            links,
            jnp.pad(
                jnp.concatenate([conv_values[layer], conv_shared[layer]], axis=1), ((0, 4), (0, 0))
            ),
            jnp.pad(heads, ((0, 6), (0, LANES - heads_row))),
            jnp.repeat(skip_gain[layer], M_HEAD)[None, :],
            spread,
        )
        sides.append(side)
    local_gains = jnp.concatenate([input_gain, post_gain], axis=0)
    spare = jnp.stack(three_parts(local_gains), axis=0).reshape(6 * LAYERS, -1).T
    first_spare = sizes[5] + heads_row
    in_first = lax.dynamic_update_slice(in_local[0], spare, (0, first_spare))
    rows, blocks = hidden_in.shape[1] // 2, lax.axis_size("col")
    in_cols, out_cols, all_ffn = in_local.shape[2], out_local.shape[2], ffn_local.shape[2]
    cut = sizes[3]
    chunks = (
        in_first[:, :cut],
        jnp.concatenate([in_first[:, cut:], out_local[0]], axis=1),
        ffn_local[0],
    )
    front, rear, ffn_first = gather_first(chunks)
    rest = in_cols - cut
    mixer_pieces = [front + rear]
    plans = [
        (
            first_plan(0, rows, (0, 0, cut)) + first_plan(5, rows, (0, cut, rest)),
            first_plan(5, rows, (rest, 0, out_cols)),
        )
    ]
    ffn_pieces, ffn_plans = [ffn_first], [first_plan(0, rows, (0, 0, all_ffn))]
    earlier = ffn_first[2]
    for layer in range(1, LAYERS):
        later = jnp.concatenate([in_local[layer], out_local[layer]], axis=1)
        mixer_pieces.append(gather_later(later, earlier))
        plans.append(
            (
                later_plan(rows, blocks, (0, 0, in_cols)),
                later_plan(rows, blocks, (in_cols, 0, out_cols)),
            )
        )
        ffn_pieces.append(gather_whole(ffn_local[layer], mixer_pieces[-1][0]))
        ffn_plans.append(whole_plan(rows, blocks, (0, 0, all_ffn)))
    spares = [piece[:, first_spare - cut : first_spare - cut + 6 * LAYERS] for piece in rear]
    mine, second, pair, theirs, others = spares
    col = lax.axis_index("col")

    def in_place(own, first, second, third):
        near, far = in_order(own, first, col & 1, 0), in_order(second, third, col & 1, 0)
        return in_order(near, far, col >> 1, 0)

    spare = jnp.concatenate(
        [
            in_place(mine, pair[:rows], second, pair[rows:]),
            in_place(theirs, others[rows : 2 * rows], others[:rows], others[2 * rows :]),
        ],
        axis=0,
    )
    gains = jnp.sum(spare.T.astype(f32).reshape(3, 2 * LAYERS, -1), axis=0)
    params = [
        (
            gains[layer : layer + 1],
            gains[LAYERS + layer : LAYERS + layer + 1],
            mixer_pieces[layer],
            plans[layer],
            ffn_pieces[layer],
            ffn_plans[layer],
            sides[layer],
            in_cols,
            all_ffn // 3,
        )
        for layer in range(LAYERS)
    ]

    hidden = whole_features(hidden_in)
    grad = whole_features(cotangent)
    stored, summed = [], ()
    for layer in range(LAYERS):
        hidden, summed, saved = layer_forward(
            hidden, summed, params[layer], sizes, (grad,) if layer == 0 else ()
        )
        stored.append(saved)
    hidden_out = hidden + in_order(*summed, row_index & 1, 0).astype(f32)
    hidden_out = own_features(hidden_out.astype(bf16))
    sums, above, waited = [None] * LAYERS, None, ((), (), None)
    heads, taps, input_gains, post_gains = [], [], [], []
    for layer in reversed(range(LAYERS)):
        above, waited, gain_above, post_gain_grad, dheads, dtaps, sums[layer] = layer_backward(
            grad, above, stored[layer], params[layer], sizes, layer, waited
        )
        if gain_above is not None:
            input_gains.insert(0, gain_above[0])
        post_gains.insert(0, post_gain_grad[0])
        heads.insert(0, dheads[:3].reshape(-1))
        taps.insert(0, dtaps[:4].reshape(-1))
    grad, last_gain = last_norm_back(*above)
    input_gains.insert(0, last_gain)
    hidden_grad = own_features(grad.astype(bf16)).astype(f32)
    small = jnp.stack(
        [
            jnp.concatenate(
                [
                    in_blocks(input_gains[layer]),
                    in_blocks(post_gains[layer]),
                    heads[layer],
                    taps[layer],
                ]
            )
            for layer in range(LAYERS)
        ]
    )
    small = sum_small(after(small, sums[0][1]))

    half, wide = gate_weight.shape[2], 2 * gate_weight.shape[2]
    collected, shared_parts = [], []
    for layer in range(LAYERS):
        if layer == LAYERS - 1:
            wide_sum, out_sum = sums[layer]
            whole = jnp.concatenate([wide_sum, sums[0][2], out_sum], axis=1)
            whole = other_half(after(whole, sums[0][3]))
            wide_part, down_part, in_part, shared_part, out_part = jnp.split(
                whole, [wide, wide + half, wide + half + sizes[3], wide + half + in_cols], axis=1
            )
        else:
            wide_sum, mixer_sum = sums[layer][:2]
            whole, mixer = other_half(wide_sum), other_half(mixer_sum)
            wide_part, down_part = whole[:, :wide], whole[:, wide:]
            in_part, shared_part, out_part = jnp.split(mixer, [sizes[3], in_cols], axis=1)
        shared_parts.append(shared_part)
        collected.append((wide_part, in_part, down_part, out_part))

    key_cols = keyval_weight.shape[2]
    placed = []
    for part in shared_parts:
        keyval = jnp.zeros((part.shape[0], key_cols), bf16)
        key_at = state_cols
        keyval = lax.dynamic_update_slice_in_dim(keyval, part[:, key_at : key_at + HEAD], key_first, 1)
        keyval = lax.dynamic_update_slice_in_dim(
            keyval, part[:, key_at + HEAD : key_at + 2 * HEAD], value_first, 1
        )
        key_at = key_at + 2 * HEAD
        steps = lax.dynamic_update_slice_in_dim(
            jnp.zeros((part.shape[0], step_weight.shape[2]), bf16),
            part[:, key_at : key_at + heads_row],
            step_first,
            1,
        )
        total = jnp.concatenate([keyval, part[:, :state_cols], steps], axis=1)
        total = add(total, swap(total, "row", 1))
        placed.append(total.astype(f32) + swap(total, "row", 2).astype(f32))
    features = hidden_in.shape[1]
    width = features * lax.axis_size("col")
    taps = small[:, 2 * width + 3 * LANES :].reshape(LAYERS, 4, input_cols + state_cols)
    heads = small[:, 2 * width : 2 * width + 3 * LANES].reshape(LAYERS, 3, LANES)

    def own_gain(first):
        return lax.dynamic_slice_in_dim(small, first + col_index * features, features, 1)

    def outputs(member, first=None, last=None, turned=False):
        entries = [entry[member].astype(f32) for entry in collected]
        if turned:
            entries = [entry.T[first:last] for entry in entries]
        else:
            entries = [entry[:, first:last] for entry in entries]
        return jnp.stack(entries)

    attn_rows = attention_out.shape[1]
    shared = jnp.stack(placed)
    return (
        hidden_out,
        hidden_grad,
        own_gain(0),
        outputs(1, 0, sizes[1]),
        shared[:, :, :key_cols],
        outputs(1, sizes[1], sizes[2]),
        outputs(1, sizes[2], sizes[3]),
        shared[:, :, key_cols : key_cols + state_cols],
        shared[:, :, key_cols + state_cols :],
        taps[:, :, :input_cols],
        sum_row_small(taps[:, :, input_cols:]),
        heads[:, 0, :heads_row],
        heads[:, 1, :heads_row],
        heads[:, 2, :heads_row],
        outputs(3, 0, attn_rows, True),
        outputs(3, attn_rows, None, True),
        own_gain(width),
        outputs(0, 0, half),
        outputs(0, half, wide),
        outputs(2, 0, None, True),
    )


def solution(mesh):
    placed = (
        P(("dp", "row"), "col"),
        P("dp"),
        P(("dp", "row"), "col"),
        P(None, "col"),
        P(None, "col", "row"),
        P(None, "col", None),
        P(None, "col", "row"),
        P(None, "col", "row"),
        P(None, "col", None),
        P(None, "col", None),
        P(None, None, "row"),
        P(),
        P(None, "row"),
        P(None, "row"),
        P(None, "row"),
        P(None, "row", "col"),
        P(None, "row", "col"),
        P(None, "col"),
        P(None, "col", "row"),
        P(None, "col", "row"),
        P(None, "row", "col"),
    )
    return jax.shard_map(
        shards,
        mesh=mesh,
        in_specs=placed,
        out_specs=(
            P(("dp", "row"), "col"),
            P(("dp", "row"), "col"),
            P(None, "col"),
            P(None, "col", "row"),
            P(None, "col", None),
            P(None, "col", "row"),
            P(None, "col", "row"),
            P(None, "col", None),
            P(None, "col", None),
            P(None, None, "row"),
            P(),
            P(None, "row"),
            P(None, "row"),
            P(None, "row"),
            P(None, "row", "col"),
            P(None, "row", "col"),
            P(None, "col"),
            P(None, "col", "row"),
            P(None, "col", "row"),
            P(None, "row", "col"),
        ),
        check_vma=False,
    )
```

```python
from functools import partial

import jax
import jax.numpy as jnp
from jax import lax
from jax.experimental import pallas as pl
from jax.experimental.pallas import tpu as pltpu
from jax.sharding import PartitionSpec as P

HEADS = 8
KV_HEADS = 2
HEAD = 64
M_HEAD = 64
LAYERS = 2
LANES = 128
ROWS = 128

epsilon = 1e-05
highest = lax.Precision.HIGHEST
f32 = jnp.float32
bf16 = jnp.bfloat16

NN = (((1,), (0,)), ((), ()))
NT = (((1,), (1,)), ((), ()))
TN = (((0,), (0,)), ((), ()))


def dot(left, right, dims=NN, precision=None):
    return lax.dot_general(left, right, dims, precision=precision, preferred_element_type=f32)


def left_lanes():
    return lax.broadcasted_iota(jnp.int32, (ROWS, LANES), 1) < HEAD


def side_lanes():
    lane = lax.broadcasted_iota(jnp.int32, (ROWS, LANES), 1)
    return lane < HEAD, lane >= HEAD


def prepare(block, sizes, proj_ref, link_ref, taps_ref, heads_ref, spread_ref):
    first, last = block * ROWS, (block + 1) * ROWS
    conv_first, conv_last, steps_first = sizes[2], sizes[4], sizes[5]
    signal = proj_ref[first:last, conv_first:conv_last]
    if block == 0:
        prior = jnp.zeros((8, conv_last - conv_first), f32)
    else:
        prior = proj_ref[first - 8 : first, conv_first:conv_last]
    joined = jnp.concatenate([prior, signal], axis=0)
    pre = signal * taps_ref[0:1, :]
    for offset in range(1, 4):
        earlier = joined[8 - offset : 8 - offset + ROWS]
        pre = pre + earlier * taps_ref[offset : offset + 1, :] * link_ref[first:last, offset : offset + 1]
    raw = proj_ref[first:last, steps_first : steps_first + LANES] + heads_ref[0:1, :]
    steps = jnp.maximum(raw, 0.0) + jnp.log1p(jnp.exp(-jnp.abs(raw)))
    wide = dot(steps, spread_ref[...], NN, highest)
    return pre, raw, steps, wide


def running(steps, heads_ref, carry):
    lower = (
        lax.broadcasted_iota(jnp.int32, (ROWS, ROWS), 0)
        >= lax.broadcasted_iota(jnp.int32, (ROWS, ROWS), 1)
    ).astype(f32)
    return dot(lower, -steps * heads_ref[1:2, :], NN, highest) + carry


def key_value(block, sizes, proj_ref):
    pair = proj_ref[block * ROWS : (block + 1) * ROWS, sizes[4] : sizes[5]]
    turned = pltpu.roll(pair, HEAD, 1)
    left = left_lanes()
    return jnp.where(left, pair, turned).astype(bf16), jnp.where(left, turned, pair).astype(bf16)


def hidden_links(block, segc_ref, segr_ref):
    width = (block + 1) * ROWS
    token = lax.broadcasted_iota(jnp.int32, (ROWS, width), 0) + block * ROWS
    source = lax.broadcasted_iota(jnp.int32, (ROWS, width), 1)
    same = segc_ref[block * ROWS : width, :] == segr_ref[:, :width]
    return jnp.where((token >= source) & same, 0.0, -1e30)


def mixer_forward_kernel(
    sizes,
    proj_ref,
    segc_ref,
    segr_ref,
    link_ref,
    taps_ref,
    heads_ref,
    skip_ref,
    spread_ref,
    out_ref,
    inner_s,
    xdt_s,
    b_s,
    c_s,
    cum_s,
    turned_s,
    key_s,
    value_s,
):
    blocks = proj_ref.shape[0] // ROWS
    width = sizes[3] - sizes[2]
    carry = jnp.zeros((1, LANES), f32)
    for block in range(blocks):
        rows = slice(block * ROWS, (block + 1) * ROWS)
        pre, raw, steps, wide = prepare(
            block, sizes, proj_ref, link_ref, taps_ref, heads_ref, spread_ref
        )
        active = pre * jax.nn.sigmoid(pre)
        inner = active[:, :width]
        inner_s[rows, :] = inner
        xdt_s[rows, :] = (inner * wide).astype(bf16)
        b_s[rows, :] = active[:, width : width + LANES].astype(bf16)
        c_s[rows, :] = active[:, width + LANES :].astype(bf16)
        cum = running(steps, heads_ref, carry)
        carry = cum[ROWS - 1 :, :]
        cum_s[rows, :] = cum
        turned_s[:, rows] = cum.T
        key_s[rows, :], value_s[rows, :] = key_value(block, sizes, proj_ref)
    left = left_lanes()
    for block in range(blocks):
        rows = slice(block * ROWS, (block + 1) * ROWS)
        span = (block + 1) * ROWS
        bias = hidden_links(block, segc_ref, segr_ref)
        query = proj_ref[rows, : sizes[1]]
        parts = []
        for side in range(2):
            chosen = jnp.where(side_lanes()[side], query, 0.0).astype(bf16)
            scores = dot(chosen, key_s[:span, :], NT) * (HEAD**-0.5) + bias
            weights = jnp.exp(scores - jnp.max(scores, axis=1, keepdims=True))
            weights = weights * (1.0 / jnp.sum(weights, axis=1, keepdims=True))
            parts.append(dot(weights.astype(bf16), value_s[:span, :]))
        out_ref[rows, : sizes[1]] = jnp.where(left, parts[0], parts[1]).astype(bf16)
        affinity = dot(c_s[rows, :], b_s[:span, :], NT)
        for pair in range(width // LANES):
            cols = slice(pair * LANES, (pair + 1) * LANES)
            parts = []
            for side in range(2):
                head = 2 * pair + side
                decay = jnp.exp(
                    cum_s[rows, head : head + 1] - turned_s[head : head + 1, :span] + bias
                )
                parts.append(dot((affinity * decay).astype(bf16), xdt_s[:span, cols]))
            scanned = jnp.where(left, parts[0], parts[1])
            scanned = scanned + skip_ref[:, cols] * inner_s[rows, cols]
            gate = proj_ref[rows, sizes[1] + pair * LANES : sizes[1] + (pair + 1) * LANES]
            out_ref[rows, sizes[1] + pair * LANES : sizes[1] + (pair + 1) * LANES] = (
                scanned * gate * jax.nn.sigmoid(gate)
            ).astype(bf16)


def mixer_backward_kernel(
    sizes,
    proj_ref,
    dmix_ref,
    segc_ref,
    segr_ref,
    link_ref,
    taps_ref,
    heads_ref,
    skip_ref,
    spread_ref,
    dproj_ref,
    dtaps_ref,
    dheads_ref,
    inner_s,
    xdt_s,
    b_s,
    c_s,
    cum_s,
    turned_s,
    key_s,
    value_s,
    pre_s,
    dscan_s,
    dxdt_s,
    db_s,
    dc_s,
    dkey_s,
    dvalue_s,
    dcum_s,
    dpre_s,
):
    length = proj_ref.shape[0]
    blocks = length // ROWS
    width = sizes[3] - sizes[2]
    conv_first, conv_last, steps_first = sizes[2], sizes[4], sizes[5]
    conv_width = conv_last - conv_first
    carry = jnp.zeros((1, LANES), f32)
    for block in range(blocks):
        rows = slice(block * ROWS, (block + 1) * ROWS)
        pre, raw, steps, wide = prepare(
            block, sizes, proj_ref, link_ref, taps_ref, heads_ref, spread_ref
        )
        pre_s[rows, :] = pre
        active = pre * jax.nn.sigmoid(pre)
        inner = active[:, :width]
        inner_s[rows, :] = inner
        xdt_s[rows, :] = (inner * wide).astype(bf16)
        b_s[rows, :] = active[:, width : width + LANES].astype(bf16)
        c_s[rows, :] = active[:, width + LANES :].astype(bf16)
        cum = running(steps, heads_ref, carry)
        carry = cum[ROWS - 1 :, :]
        cum_s[rows, :] = cum
        turned_s[:, rows] = cum.T
        key_s[rows, :], value_s[rows, :] = key_value(block, sizes, proj_ref)
    dxdt_s[...] = jnp.zeros_like(dxdt_s)
    db_s[...] = jnp.zeros_like(db_s)
    dkey_s[...] = jnp.zeros_like(dkey_s)
    dvalue_s[...] = jnp.zeros_like(dvalue_s)
    left = left_lanes()
    dskip = jnp.zeros((1, width), f32)
    for block in range(blocks):
        rows = slice(block * ROWS, (block + 1) * ROWS)
        span = (block + 1) * ROWS
        bias = hidden_links(block, segc_ref, segr_ref)
        query = proj_ref[rows, : sizes[1]]
        dattended = dmix_ref[rows, : sizes[1]]
        parts = []
        for side in range(2):
            own = side_lanes()[side]
            chosen = jnp.where(own, query, 0.0).astype(bf16)
            dchosen = jnp.where(own, dattended, 0.0).astype(bf16)
            scores = dot(chosen, key_s[:span, :], NT) * (HEAD**-0.5) + bias
            weights = jnp.exp(scores - jnp.max(scores, axis=1, keepdims=True))
            weights = weights * (1.0 / jnp.sum(weights, axis=1, keepdims=True))
            dweights = dot(dchosen, value_s[:span, :], NT)
            dvalue_s[:span, :] += dot(weights.astype(bf16), dchosen, TN)
            mean = jnp.sum(weights * dweights, axis=1, keepdims=True)
            dscores = (weights * (dweights - mean) * (HEAD**-0.5)).astype(bf16)
            parts.append(dot(dscores, key_s[:span, :]))
            dkey_s[:span, :] += dot(dscores, chosen, TN)
        dproj_ref[rows, : sizes[1]] = jnp.where(left, parts[0], parts[1]).astype(bf16)
        affinity = dot(c_s[rows, :], b_s[:span, :], NT)
        daffinity = jnp.zeros((ROWS, span), f32)
        dcum = jnp.zeros((ROWS, LANES), f32)
        for pair in range(width // LANES):
            cols = slice(pair * LANES, (pair + 1) * LANES)
            gate_cols = slice(sizes[1] + pair * LANES, sizes[1] + (pair + 1) * LANES)
            gate = proj_ref[rows, gate_cols]
            lifted = jax.nn.sigmoid(gate)
            dmamba = dmix_ref[rows, gate_cols]
            dscan = dmamba * gate * lifted
            dscan_s[rows, cols] = dscan
            parts, mixes, sides = [], [], []
            for side in range(2):
                head = 2 * pair + side
                decay = jnp.exp(
                    cum_s[rows, head : head + 1] - turned_s[head : head + 1, :span] + bias
                )
                mix = (affinity * decay).astype(bf16)
                dside = jnp.where(side_lanes()[side], dscan, 0.0).astype(bf16)
                daffinity = daffinity + dot(dside, xdt_s[:span, cols], NT) * decay
                parts.append(dot(mix, xdt_s[:span, cols]))
                mixes.append(mix)
                sides.append(dside)
            dxdt_s[:span, cols] += dot(
                jnp.concatenate(mixes, axis=0), jnp.concatenate(sides, axis=0), TN
            )
            scanned = jnp.where(left, parts[0], parts[1])
            inner = inner_s[rows, cols]
            dcum = dcum + dot(
                scanned * dscan.astype(bf16).astype(f32), spread_ref[:, cols], NT, highest
            )
            scanned = scanned + skip_ref[:, cols] * inner
            dproj_ref[rows, gate_cols] = (
                dmamba * scanned * lifted * (1.0 + gate * (1.0 - lifted))
            ).astype(bf16)
        dcum_s[rows, :] = dcum
        dskip = dskip + jnp.sum(dscan_s[rows, :] * inner_s[rows, :], axis=0, keepdims=True)
        daffinity = daffinity.astype(bf16)
        dc_s[rows, :] = dot(daffinity, b_s[:span, :])
        db_s[:span, :] += dot(daffinity, c_s[rows, :], TN)
    upper = (
        lax.broadcasted_iota(jnp.int32, (ROWS, ROWS), 0)
        <= lax.broadcasted_iota(jnp.int32, (ROWS, ROWS), 1)
    ).astype(f32)
    carry = jnp.zeros((1, LANES), f32)
    dbias = jnp.zeros((1, LANES), f32)
    drate = jnp.zeros((1, LANES), f32)
    dpre_s[length:, :] = jnp.zeros((8, conv_width), f32)
    for block in reversed(range(blocks)):
        rows = slice(block * ROWS, (block + 1) * ROWS)
        raw = proj_ref[rows, steps_first : steps_first + LANES] + heads_ref[0:1, :]
        steps = jnp.maximum(raw, 0.0) + jnp.log1p(jnp.exp(-jnp.abs(raw)))
        wide = dot(steps, spread_ref[...], NN, highest)
        dxdt = dxdt_s[rows, :]
        dcum = dcum_s[rows, :] - dot(
            xdt_s[rows, :].astype(f32) * dxdt, spread_ref[...], NT, highest
        )
        dlog = dot(upper, dcum, NN, highest) + carry
        carry = dlog[0:1, :]
        dsteps = (
            dot(dxdt * inner_s[rows, :], spread_ref[...], NT, highest) - heads_ref[1:2, :] * dlog
        )
        drate = drate - jnp.sum(steps * dlog, axis=0, keepdims=True)
        draw = dsteps * jax.nn.sigmoid(raw)
        dbias = dbias + jnp.sum(draw, axis=0, keepdims=True)
        dproj_ref[rows, steps_first : steps_first + LANES] = draw.astype(bf16)
        dinner = dxdt * wide + skip_ref[...] * dscan_s[rows, :]
        dactive = jnp.concatenate([dinner, db_s[rows, :], dc_s[rows, :]], axis=1)
        pre = pre_s[rows, :]
        lifted = jax.nn.sigmoid(pre)
        dpre_s[rows, :] = dactive * lifted * (1.0 + pre * (1.0 - lifted))
        dkey = dkey_s[rows, :]
        dvalue = dvalue_s[rows, :]
        dkey = dkey + pltpu.roll(dkey, HEAD, 1)
        dvalue = dvalue + pltpu.roll(dvalue, HEAD, 1)
        dproj_ref[rows, conv_last:steps_first] = jnp.where(left, dkey, dvalue).astype(bf16)
    dtaps = [jnp.zeros((1, conv_width), f32) for _ in range(4)]
    for block in range(blocks):
        first, last = block * ROWS, (block + 1) * ROWS
        signal = proj_ref[first:last, conv_first:conv_last]
        joined = dpre_s[first : last + 8, :]
        own = joined[:ROWS]
        dsignal = own * taps_ref[0:1, :]
        dtaps[0] = dtaps[0] + jnp.sum(signal * own, axis=0, keepdims=True)
        for offset in range(1, 4):
            later = (joined * link_ref[first : last + 8, offset : offset + 1])[
                offset : offset + ROWS
            ]
            dsignal = dsignal + later * taps_ref[offset : offset + 1, :]
            dtaps[offset] = dtaps[offset] + jnp.sum(signal * later, axis=0, keepdims=True)
        dproj_ref[first:last, conv_first:conv_last] = dsignal.astype(bf16)
    dtaps_ref[...] = jnp.concatenate(dtaps + [jnp.zeros((4, conv_width), f32)], axis=0)
    dheads_ref[...] = jnp.concatenate(
        [
            dbias,
            drate * heads_ref[1:2, :],
            dot(dskip, spread_ref[...], NT, highest),
            jnp.zeros((5, LANES), f32),
        ],
        axis=0,
    )


def shared_scratch(length, width):
    return [
        pltpu.VMEM((length, width), f32),
        pltpu.VMEM((length, width), bf16),
        pltpu.VMEM((length, LANES), bf16),
        pltpu.VMEM((length, LANES), bf16),
        pltpu.VMEM((length, LANES), f32),
        pltpu.VMEM((LANES, length), f32),
        pltpu.VMEM((length, LANES), bf16),
        pltpu.VMEM((length, LANES), bf16),
    ]


def fetch(plan, refs, target, semaphores):
    col = lax.axis_index("col")
    whole = target.shape[0] // 2
    copies = []
    for index, (piece, first, rows, half, distance, source, place, count) in enumerate(plan):
        if isinstance(half, tuple):
            at = pl.multiple_of((half[0] ^ (lax.axis_index("dp") & 1)) * whole, rows)
        else:
            at = half * whole
        if isinstance(distance, tuple):
            at = pl.multiple_of(at + distance[0] * rows, rows)
        elif distance is not None:
            at = pl.multiple_of(at + (col ^ distance) * rows, rows)
        copy = pltpu.make_async_copy(
            refs[piece].at[pl.ds(first, rows), pl.ds(source, count)],
            target.at[pl.ds(at, rows), pl.ds(place, count)],
            semaphores.at[index],
        )
        copy.start()
        copies.append(copy)
    return copies


def arrived(copies):
    for copy in copies:
        copy.wait()


def own_rows(length):
    half = length // 2
    parity = lax.axis_index("row") & 1
    return (
        pl.ds(pl.multiple_of(parity * half, half), half),
        pl.ds(pl.multiple_of((1 - parity) * half, half), half),
    )


def by_rows(length, body):
    def step(index, carry):
        body(pl.ds(pl.multiple_of(index * ROWS, ROWS), ROWS))
        return carry

    lax.fori_loop(0, length // ROWS, step, 0)


def add_sum(base_ref, sum_refs, total_ref):
    for rows, part in zip(own_rows(base_ref.shape[0]), sum_refs):
        total_ref[rows, :] = base_ref[rows, :] + part[...].astype(f32)


def norm_rows(hidden_ref, gain_ref, normed_ref):
    def body(rows):
        hidden = hidden_ref[rows, :]
        inverse = lax.rsqrt(jnp.mean(hidden * hidden, axis=1, keepdims=True) + epsilon)
        normed_ref[rows, :] = (hidden * inverse * gain_ref[...]).astype(bf16)

    by_rows(hidden_ref.shape[0], body)


def norm_back_rows(hidden_ref, gain_ref, grad_ref, base_ref, total_ref, low_ref, dgain_ref):
    dgain_ref[...] = jnp.zeros_like(dgain_ref)

    def body(rows):
        hidden, grad = hidden_ref[rows, :], grad_ref[rows, :].astype(f32)
        inverse = lax.rsqrt(jnp.mean(hidden * hidden, axis=1, keepdims=True) + epsilon)
        weighted = grad * gain_ref[...]
        mean = jnp.mean(weighted * hidden, axis=1, keepdims=True)
        total = base_ref[rows, :] + (
            inverse * weighted - hidden * (inverse * inverse * inverse * mean)
        )
        total_ref[rows, :] = total
        low_ref[rows, :] = total.astype(bf16)
        dgain_ref[...] += jnp.sum(grad * hidden * inverse, axis=0, keepdims=True)

    by_rows(hidden_ref.shape[0], body)


def set_sum(sum_refs, total_ref):
    for rows, part in zip(own_rows(total_ref.shape[0]), sum_refs):
        total_ref[rows, :] = part[...]


def times(left_ref, weight_ref, first, last, result_ref, place=0, dims=NN):
    for column in range(first, last, 256):
        count = min(256, last - column)
        result_ref[:, place + column - first : place + column - first + count] = dot(
            left_ref[...], weight_ref[:, column : column + count]
        ).astype(result_ref.dtype)


def parts(left_ref, weight_ref, first, last, kept_ref, away_ref):
    for rows, part_ref in zip(own_rows(left_ref.shape[0]), (kept_ref, away_ref)):
        left = left_ref[rows, :]
        for feature in range(0, weight_ref.shape[0], 256):
            part_ref[:, feature : feature + 256] = dot(
                left, weight_ref[feature : feature + 256, first:last], NT
            ).astype(bf16)


def take(refs, *counts):
    taken = []
    for count in counts:
        taken.append(refs[:count])
        refs = refs[count:]
    return taken


def first_kernel(sizes, plans, counts, *refs):
    ins, outs, scratch = take(refs, *counts[:3])
    summed = len(ins) - counts[3] - 9 == 2
    base_ref, gain_ref = ins[:2]
    side = ins[2:9]
    sums, pieces = ins[9 : len(ins) - counts[3]], ins[len(ins) - counts[3] :]
    hidden_ref, normed_ref, proj_ref, mixed_ref, kept_ref, away_ref = outs
    in_ref, out_ref, in_sems, out_sems = scratch[:4]
    waits = fetch(plans[0], pieces, in_ref, in_sems)
    out_waits = fetch(plans[1], pieces, out_ref, out_sems)
    if summed:
        add_sum(base_ref, sums, hidden_ref)
    else:
        hidden_ref[...] = base_ref[...].astype(f32)
    norm_rows(hidden_ref, gain_ref, normed_ref)
    arrived(waits)
    times(normed_ref, in_ref, 0, in_ref.shape[1], proj_ref)
    mixer_forward_kernel(sizes, proj_ref, *side, mixed_ref, *scratch[4:])
    arrived(out_waits)
    parts(mixed_ref, out_ref, 0, out_ref.shape[1], kept_ref, away_ref)


def second_kernel(plans, counts, *refs):
    ins, outs, scratch = take(refs, *counts[:3])
    hidden_ref, gain_ref, kept_sum, other_sum = ins[:4]
    middle_ref, post_ref, wide_ref, active_ref, kept_ref, away_ref = outs
    ffn_ref, sems = scratch
    waits = fetch(plans[0], ins[4:], ffn_ref, sems)
    add_sum(hidden_ref, (kept_sum, other_sum), middle_ref)
    norm_rows(middle_ref, gain_ref, post_ref)
    arrived(waits)
    half = ffn_ref.shape[1] // 3
    times(post_ref, ffn_ref, 0, 2 * half, wide_ref)

    def body(rows):
        gate, upper = wide_ref[rows, :half], wide_ref[rows, half:]
        active_ref[rows, :] = (gate * jax.nn.sigmoid(gate) * upper).astype(bf16)

    by_rows(wide_ref.shape[0], body)
    parts(active_ref, ffn_ref, 2 * half, 3 * half, kept_ref, away_ref)


def third_kernel(plans, counts, *refs):
    ins, outs, scratch = take(refs, *counts[:3])
    ffn_ref, sems, dactive_ref = scratch[:3]
    wide_ref = ins[0]
    pieces = ins[len(ins) - counts[3] :]
    waits = fetch(plans[0], pieces, ffn_ref, sems)
    low_ref, dwide_ref, kept_ref, away_ref = outs[:4]
    if len(outs) == 6:
        hidden_ref, gain_ref, base_ref, kept_sum, other_sum = ins[1:6]
        grad_ref, dgain_ref = outs[4:]
        dnormed_ref = scratch[3]
        set_sum((kept_sum, other_sum), dnormed_ref)
        norm_back_rows(hidden_ref, gain_ref, dnormed_ref, base_ref, grad_ref, low_ref, dgain_ref)
    else:
        low_ref[...] = ins[1][...].astype(bf16)
    arrived(waits)
    half = ffn_ref.shape[1] // 3
    times(low_ref, ffn_ref, 2 * half, 3 * half, dactive_ref)

    def body(rows):
        gate, upper = wide_ref[rows, :half], wide_ref[rows, half:]
        dactive = dactive_ref[rows, :]
        lifted = jax.nn.sigmoid(gate)
        dwide_ref[rows, :half] = (
            dactive * upper * lifted * (1.0 + gate * (1.0 - lifted))
        ).astype(bf16)
        dwide_ref[rows, half:] = (dactive * gate * lifted).astype(bf16)

    by_rows(wide_ref.shape[0], body)
    parts(dwide_ref, ffn_ref, 0, 2 * half, kept_ref, away_ref)


def fourth_kernel(sizes, plans, counts, *refs):
    ins, outs, scratch = take(refs, *counts[:3])
    base_ref, middle_ref, gain_ref, kept_sum, other_sum, proj_ref = ins[:6]
    side = ins[6:13]
    pieces = ins[len(ins) - counts[3] :]
    dmiddle_ref, low_ref, dgain_ref, dproj_ref, dtaps_ref, dheads_ref, kept_ref, away_ref = outs
    in_ref, out_ref, in_sems, out_sems, dpost_ref, dmix_ref = scratch[:6]
    out_waits = fetch(plans[1], pieces, out_ref, out_sems)
    waits = fetch(plans[0], pieces, in_ref, in_sems)
    set_sum((kept_sum, other_sum), dpost_ref)
    norm_back_rows(middle_ref, gain_ref, dpost_ref, base_ref, dmiddle_ref, low_ref, dgain_ref)
    arrived(out_waits)
    times(low_ref, out_ref, 0, out_ref.shape[1], dmix_ref)
    mixer_backward_kernel(
        sizes, proj_ref, dmix_ref, *side, dproj_ref, dtaps_ref, dheads_ref, *scratch[6:]
    )
    arrived(waits)
    parts(dproj_ref, in_ref, 0, in_ref.shape[1], kept_ref, away_ref)


def run_kernel(kernel, name, ins, pieces, out_shapes, scratch, waited=(), flops=10**9):
    vmem, anywhere = pl.BlockSpec(memory_space=pltpu.VMEM), pl.BlockSpec(memory_space=pl.ANY)
    arrays = list(ins) + list(waited) + list(pieces)
    counts = (len(arrays), len(out_shapes), len(scratch), len(pieces) + len(waited))

    def body(*refs):
        ordered = list(refs)
        first = len(ins)
        ordered[first : first + len(waited) + len(pieces)] = (
            refs[first + len(waited) : len(arrays)] + refs[first : first + len(waited)]
        )
        kernel(counts, *ordered)

    return pl.pallas_call(
        body,
        out_shape=out_shapes,
        in_specs=[vmem] * len(ins) + [anywhere] * (len(waited) + len(pieces)),
        out_specs=[vmem] * len(out_shapes),
        scratch_shapes=scratch,
        compiler_params=pltpu.CompilerParams(vmem_limit_bytes=56 * 1024 * 1024),
        cost_estimate=pl.CostEstimate(
            flops=flops, bytes_accessed=10**7, transcendentals=10**6
        ),
        name=name,
    )(*arrays)


def shape(kind, *sizes):
    return jax.ShapeDtypeStruct(sizes, kind)


def swap(value, axis, distance):
    size = lax.axis_size(axis)
    return lax.ppermute(value, axis, [(i, i ^ distance) for i in range(size)])


def after(value, other):
    last = tuple(size - 1 for size in other.shape)
    ready = jnp.logical_not(other[last].astype(f32) > 3.3e38)
    return jnp.where(ready, value, jnp.zeros_like(value))


def bound(value, *others):
    for other in others:
        value = after(value, other)
    return value


def add(left, right):
    return (left.astype(f32) + right.astype(f32)).astype(bf16)


def row_steps(kept, away):
    middle = add(kept, swap(away, "row", 1))
    kept = add(middle, swap(middle, "row", 2))
    return middle, (kept, swap(kept, "row", 1))


def row_sum(kept, away):
    return row_steps(kept, away)[1]


def in_order(own, other, own_is_second, axis):
    return jnp.where(
        own_is_second == 0,
        jnp.concatenate([own, other], axis=axis),
        jnp.concatenate([other, own], axis=axis),
    )


def half_index():
    return lax.axis_index("dp") & 1


def turn(value, axis):
    low, high = jnp.split(value, 2, axis=axis)
    return in_order(low, high, half_index(), axis)


def by_half(value):
    pieces = jnp.split(value, value.shape[1] // LANES, axis=1)
    return jnp.concatenate(pieces[0::2] + pieces[1::2], axis=1)


def by_block(value):
    count = value.shape[1] // LANES // 2
    pieces = jnp.split(value, 2 * count, axis=1)
    return jnp.concatenate(
        [pieces[half * count + block] for block in range(count) for half in range(2)], axis=1
    )


def transpose_blocks(value):
    rows, cols = lax.axis_size("row"), lax.axis_size("col")
    pairs = [(r * cols + c, c * cols + r) for r in range(rows) for c in range(cols)]
    return lax.ppermute(value, ("row", "col"), pairs)


def whole_features(value):
    block = transpose_blocks(turn(value, 1))
    row = lax.axis_index("row")
    pair = in_order(block, swap(block, "row", 1), row & 1, 1)
    return by_half(in_order(pair, swap(pair, "row", 2), row >> 1, 1))


def own_features(value):
    row = lax.axis_index("row")
    halves = [
        lax.dynamic_slice_in_dim(piece, row * LANES, LANES, 1)
        for piece in jnp.split(value, 2, axis=1)
    ]
    return transpose_blocks(turn(jnp.concatenate(halves, axis=1), 1))


def gather_first(chunks):
    halves = [jnp.split(turn(chunk, 0), 2, axis=0) for chunk in chunks]
    gathered, seconds, earlier = [], [], None
    for mine, _ in halves:
        if earlier is not None:
            mine = after(mine, earlier)
        seconds.append(swap(mine, "col", 2))
        earlier = seconds[-1]
    for (mine, theirs), second in zip(halves, seconds):
        pair = swap(jnp.concatenate([mine, second], axis=0), "col", 1)
        others = swap(jnp.concatenate([second, pair], axis=0), "dp", 1)
        gathered.append((mine, second, pair, theirs, others))
    return gathered


def first_plan(base, rows, columns):
    places = [(0, 0, 0, 0), (2, 0, 0, 1), (1, 0, 0, 2), (2, rows, 0, 3)]
    places += [(3, 0, 1, 0), (4, rows, 1, 1), (4, 0, 1, 2), (4, 2 * rows, 1, 3)]
    return [(base + piece, first, rows, half, distance, *columns) for piece, first, half, distance in places]


def gather_later(weight, earlier):
    half = weight.shape[0] // 2
    mine, theirs = jnp.split(turn(weight, 0), 2, axis=0)
    whole = lax.all_gather(after(mine, earlier), "col", axis=0, tiled=True)
    col = lax.axis_index("col")
    others = [lax.dynamic_slice_in_dim(whole, (col ^ k) * half, half, 0) for k in range(1, 4)]
    return (whole, theirs, swap(jnp.concatenate(others, axis=0), "dp", 1))


def later_plan(rows, blocks, columns):
    places = [(0, 0, rows * blocks, 0, None), (1, 0, rows, 1, 0)]
    places += [(2, (k - 1) * rows, rows, 1, k) for k in range(1, 4)]
    return [(*place, *columns) for place in places]


def gather_whole(weight, earlier):
    return (lax.all_gather(after(weight, earlier), "col", axis=0, tiled=True),)


def whole_plan(rows, blocks, columns):
    return [
        (0, (2 * block + half) * rows, rows, (half,), (block,), *columns)
        for block in range(blocks)
        for half in range(2)
    ]


def three_parts(value):
    high = lax.reduce_precision(value, 8, 7)
    rest = value - high
    middle = lax.reduce_precision(rest, 8, 7)
    return [high.astype(bf16), middle.astype(bf16), (rest - middle).astype(bf16)]


def other_batches(value):
    size = lax.axis_size("dp")
    if size == 2:
        return value
    groups = [list(range(0, size, 2)), list(range(1, size, 2))]
    return lax.psum(value, "dp", axis_index_groups=groups)


def col_scatter(value):
    return other_batches(lax.psum_scatter(value, "col", scatter_dimension=0, tiled=True))


def add_kernel(counts, *refs):
    ins, outs, _ = take(refs, *counts[:3])

    def body(rows):
        outs[0][rows, :] = (ins[0][rows, :].astype(f32) + ins[1][rows, :].astype(f32)).astype(bf16)

    by_rows(outs[0].shape[0], body)


def dp_sum(mine, received, *waited):
    outs = (jax.ShapeDtypeStruct(mine.shape, bf16),)
    return run_kernel(add_kernel, "sum_halves", (mine, received), (), outs, [], waited)[0]


def sum_batches(value):
    return add(value, swap(value, "dp", 1))


def other_half(value):
    return in_order(value, swap(value, "dp", 1), half_index(), 0)


def sum_small(value):
    value = value + swap(value, "col", 1)
    value = value + swap(value, "col", 2)
    if lax.axis_size("dp") != 2:
        return lax.psum(value, "dp")
    return value + swap(value, "dp", 1)


def sum_row_small(value):
    value = value + swap(value, "row", 1)
    return value + swap(value, "row", 2)


def in_blocks(value):
    value = value.reshape(2, -1, LANES)
    value = jnp.where(half_index() == 0, value, value[::-1])
    return jnp.swapaxes(value, 0, 1).reshape(-1)


def mixer_scratch(plan, out_plan, features, in_cols, out_cols):
    return [
        pltpu.VMEM((features, in_cols), bf16),
        pltpu.VMEM((features, out_cols), bf16),
        pltpu.SemaphoreType.DMA((len(plan),)),
        pltpu.SemaphoreType.DMA((len(out_plan),)),
    ]


def layer_forward(base, sums, params, sizes, waited):
    input_gain, post_gain, mixer_pieces, plans, ffn_pieces, ffn_plan, side, in_cols, ffn_cols = params
    length, features = base.shape
    out_cols, width = sizes[2], sizes[3] - sizes[2]
    part = shape(bf16, length // 2, features)
    hidden, normed, proj, mixed, kept, away = run_kernel(
        partial(first_kernel, sizes, plans),
        "norm_mixer_out",
        (base, input_gain, *side, *sums),
        mixer_pieces,
        (
            shape(f32, length, features),
            shape(bf16, length, features),
            shape(f32, length, in_cols),
            shape(bf16, length, out_cols),
            part,
            part,
        ),
        mixer_scratch(*plans, features, in_cols, out_cols) + shared_scratch(length, width),
        waited,
        flops=10**7,
    )
    middle, post, wide, active, kept, away = run_kernel(
        partial(second_kernel, (ffn_plan,)),
        "norm_feed_forward",
        (hidden, post_gain, *row_sum(kept, away)),
        ffn_pieces,
        (
            shape(f32, length, features),
            shape(bf16, length, features),
            shape(f32, length, 2 * ffn_cols),
            shape(bf16, length, ffn_cols),
            part,
            part,
        ),
        [
            pltpu.VMEM((features, 3 * ffn_cols), bf16),
            pltpu.SemaphoreType.DMA((len(ffn_plan),)),
        ],
        flops=2 * 10**9,
    )
    return middle, row_sum(kept, away), (hidden, normed, proj, mixed, middle, post, wide, active)


def layer_backward(grad, above, saved, params, sizes, layer, waited):
    input_gain, post_gain, mixer_pieces, plans, ffn_pieces, ffn_plan, side, in_cols, ffn_cols = params
    hidden, normed, proj, mixed, middle, post, wide, active = saved
    length, features = hidden.shape
    own = features // 2
    out_cols, width, conv_width = sizes[2], sizes[3] - sizes[2], sizes[4] - sizes[2]
    part = shape(bf16, length // 2, features)
    outs = [shape(bf16, length, features), shape(bf16, length, 2 * ffn_cols), part, part]
    scratch = [
        pltpu.VMEM((features, 3 * ffn_cols), bf16),
        pltpu.SemaphoreType.DMA((len(ffn_plan),)),
        pltpu.VMEM((length, ffn_cols), f32),
    ]
    if above is None:
        ins = (wide, grad)
    else:
        ins = (wide, *above)
        outs += [shape(f32, length, features), shape(f32, 1, features)]
        scratch.append(pltpu.VMEM((length, features), bf16))
    low, dwide, kept, away, *rest = run_kernel(
        partial(third_kernel, (ffn_plan,)),
        "feed_forward_back",
        ins,
        ffn_pieces,
        tuple(outs),
        scratch,
        waited[0],
        flops=2 * 10**9,
    )
    gain_above = None
    if above is not None:
        grad, gain_above = rest
    total = row_sum(kept, away)
    last = layer == LAYERS - 1
    theirs = jnp.concatenate(
        [
            dot(post[:, own:], dwide, TN).astype(bf16),
            dot(low[:, own:], active, TN).astype(bf16),
        ],
        axis=1,
    )
    mine = jnp.concatenate(
        [
            dot(post[:, :own], dwide, TN).astype(bf16),
            dot(low[:, :own], active, TN).astype(bf16),
        ],
        axis=1,
    )
    wide_mine, wide_received, wide_tie = mine, swap(theirs, "dp", 1), total[1]
    before = (mine, theirs) + tuple(waited[1])
    if not last:
        later = add(waited[2][0], after(waited[2][1], total[1]))
        later_sum = col_scatter(later)
        before += (later,)
    dmiddle, low, post_gain_grad, dproj, dtaps, dheads, kept, away = run_kernel(
        partial(fourth_kernel, sizes, plans),
        "norm_mixer_back",
        (grad, middle, post_gain, *total, proj, *side),
        mixer_pieces,
        (
            shape(f32, length, features),
            shape(bf16, length, features),
            shape(f32, 1, features),
            shape(bf16, length, in_cols),
            shape(f32, 8, conv_width),
            shape(f32, 8, LANES),
            part,
            part,
        ),
        mixer_scratch(*plans, features, in_cols, out_cols)
        + [pltpu.VMEM((length, features), bf16), pltpu.VMEM((length, out_cols), f32)]
        + shared_scratch(length, width)
        + [
            pltpu.VMEM((length, conv_width), f32),
            pltpu.VMEM((length, width), f32),
            pltpu.VMEM((length, width), f32),
            pltpu.VMEM((length, LANES), f32),
            pltpu.VMEM((length, LANES), f32),
            pltpu.VMEM((length, LANES), f32),
            pltpu.VMEM((length, LANES), f32),
            pltpu.VMEM((length, LANES), f32),
            pltpu.VMEM((length + 8, conv_width), f32),
        ],
        before,
        flops=5 * 10**9,
    )
    total = row_sum(kept, away)
    if last:
        wide = add(wide_mine, after(wide_received, wide_tie))
        theirs_out = dot(low[:, own:], mixed, TN).astype(bf16)
        out_received = swap(theirs_out, "dp", 1)
        mine_out = dot(low[:, :own], mixed, TN).astype(bf16)
        out = add(mine_out, after(out_received, total[0]))
        theirs = dot(normed[:, own:], dproj, TN).astype(bf16)
        mine = dot(normed[:, :own], dproj, TN).astype(bf16)
        in_received = swap(theirs, "dp", 1)
        wide_sum, out_sum = col_scatter(wide), col_scatter(out)
        waited = ((theirs, mine, wide, out), (wide_sum,), (mine, in_received))
        sums = (wide_sum, out_sum)
    else:
        theirs = jnp.concatenate(
            [
                dot(normed[:, own:], dproj, TN).astype(bf16),
                dot(low[:, own:], mixed, TN).astype(bf16),
            ],
            axis=1,
        )
        received = swap(theirs, "dp", 1)
        mine = jnp.concatenate(
            [
                dot(normed[:, :own], dproj, TN).astype(bf16),
                dot(low[:, :own], mixed, TN).astype(bf16),
            ],
            axis=1,
        )
        whole = dp_sum(mine, received, total[0], later_sum)
        whole_sum = col_scatter(whole)
        wide = dp_sum(wide_mine, wide_received, whole_sum)
        sums = (col_scatter(wide), whole_sum, later_sum, wide)
    above = (hidden, input_gain, dmiddle, *total)
    return above, waited, gain_above, post_gain_grad, dheads, dtaps, sums


def last_norm_back(hidden, gain, base, kept, other):
    grad = in_order(kept, other, lax.axis_index("row") & 1, 0).astype(f32)
    inverse = lax.rsqrt(jnp.mean(hidden * hidden, axis=1, keepdims=True) + epsilon)
    weighted = grad * gain
    mean = jnp.mean(weighted * hidden, axis=1, keepdims=True)
    total = base + inverse * weighted - hidden * (inverse * inverse * inverse * mean)
    return total, jnp.sum(grad * hidden * inverse, axis=0)


def shards(
    hidden_in,
    segments,
    cotangent,
    input_gain,
    query_weight,
    keyval_weight,
    mixer_gate_weight,
    mixer_input_weight,
    state_weight,
    step_weight,
    conv_values,
    conv_shared,
    step_bias,
    decay_log,
    skip_gain,
    attention_out,
    mixer_out,
    post_gain,
    gate_weight,
    up_weight,
    down_weight,
):
    tokens = hidden_in.shape[0]
    row_index = lax.axis_index("row")
    col_index = lax.axis_index("col")
    query_cols = query_weight.shape[2]
    gate_cols = mixer_gate_weight.shape[2]
    input_cols = mixer_input_weight.shape[2]
    state_cols = state_weight.shape[2]
    heads_row = step_bias.shape[1]
    sizes = [0]
    for count in (query_cols, gate_cols, input_cols, state_cols, 2 * HEAD):
        sizes.append(sizes[-1] + count)
    sizes = tuple(sizes)
    kv_index = row_index * (query_cols // HEAD) // (HEADS // KV_HEADS)
    key_first = kv_index * HEAD
    value_first = KV_HEADS * HEAD + kv_index * HEAD
    step_first = row_index * heads_row

    in_local = jnp.concatenate(
        [
            query_weight,
            mixer_gate_weight,
            mixer_input_weight,
            state_weight,
            lax.dynamic_slice_in_dim(keyval_weight, key_first, HEAD, 2),
            lax.dynamic_slice_in_dim(keyval_weight, value_first, HEAD, 2),
            lax.dynamic_slice_in_dim(step_weight, step_first, heads_row, 2),
            jnp.zeros(step_weight.shape[:2] + (LANES - heads_row,), bf16),
        ],
        axis=2,
    )
    out_local = jnp.swapaxes(jnp.concatenate([attention_out, mixer_out], axis=1), 1, 2)
    ffn_local = jnp.concatenate([gate_weight, up_weight, jnp.swapaxes(down_weight, 1, 2)], axis=2)

    segment_ids = lax.dynamic_slice_in_dim(segments, col_index * tokens, tokens, 0)
    links = [jnp.ones((tokens,), f32)]
    for offset in range(1, 4):
        earlier = jnp.concatenate([jnp.full((offset,), -1, jnp.int32), segment_ids[:-offset]])
        links.append((earlier == segment_ids).astype(f32))
    links = jnp.pad(jnp.stack(links, axis=1), ((0, 8), (0, 4)))
    spread = (
        lax.broadcasted_iota(jnp.int32, (LANES, heads_row * M_HEAD), 0)
        == lax.broadcasted_iota(jnp.int32, (LANES, heads_row * M_HEAD), 1) // M_HEAD
    ).astype(f32)

    sides = []
    for layer in range(LAYERS):
        heads = jnp.stack([step_bias[layer], jnp.exp(decay_log[layer])])
        side = (
            segment_ids[:, None],
            segment_ids[None, :],
            links,
            jnp.pad(
                jnp.concatenate([conv_values[layer], conv_shared[layer]], axis=1), ((0, 4), (0, 0))
            ),
            jnp.pad(heads, ((0, 6), (0, LANES - heads_row))),
            jnp.repeat(skip_gain[layer], M_HEAD)[None, :],
            spread,
        )
        sides.append(side)
    local_gains = jnp.concatenate([input_gain, post_gain], axis=0)
    spare = jnp.stack(three_parts(local_gains), axis=0).reshape(6 * LAYERS, -1).T
    first_spare = sizes[5] + heads_row
    in_first = lax.dynamic_update_slice(in_local[0], spare, (0, first_spare))
    rows, blocks = hidden_in.shape[1] // 2, lax.axis_size("col")
    in_cols, out_cols, all_ffn = in_local.shape[2], out_local.shape[2], ffn_local.shape[2]
    cut = sizes[3]
    chunks = (
        in_first[:, :cut],
        jnp.concatenate([in_first[:, cut:], out_local[0]], axis=1),
        ffn_local[0],
    )
    front, rear, ffn_first = gather_first(chunks)
    rest = in_cols - cut
    mixer_pieces = [front + rear]
    plans = [
        (
            first_plan(0, rows, (0, 0, cut)) + first_plan(5, rows, (0, cut, rest)),
            first_plan(5, rows, (rest, 0, out_cols)),
        )
    ]
    ffn_pieces, ffn_plans = [ffn_first], [first_plan(0, rows, (0, 0, all_ffn))]
    earlier = ffn_first[2]
    for layer in range(1, LAYERS):
        later = jnp.concatenate([in_local[layer], out_local[layer]], axis=1)
        mixer_pieces.append(gather_later(later, earlier))
        plans.append(
            (
                later_plan(rows, blocks, (0, 0, in_cols)),
                later_plan(rows, blocks, (in_cols, 0, out_cols)),
            )
        )
        ffn_pieces.append(gather_whole(ffn_local[layer], mixer_pieces[-1][0]))
        ffn_plans.append(whole_plan(rows, blocks, (0, 0, all_ffn)))
    spares = [piece[:, first_spare - cut : first_spare - cut + 6 * LAYERS] for piece in rear]
    mine, second, pair, theirs, others = spares
    col = lax.axis_index("col")

    def in_place(own, first, second, third):
        near, far = in_order(own, first, col & 1, 0), in_order(second, third, col & 1, 0)
        return in_order(near, far, col >> 1, 0)

    spare = jnp.concatenate(
        [
            in_place(mine, pair[:rows], second, pair[rows:]),
            in_place(theirs, others[rows : 2 * rows], others[:rows], others[2 * rows :]),
        ],
        axis=0,
    )
    gains = jnp.sum(spare.T.astype(f32).reshape(3, 2 * LAYERS, -1), axis=0)
    params = [
        (
            gains[layer : layer + 1],
            gains[LAYERS + layer : LAYERS + layer + 1],
            mixer_pieces[layer],
            plans[layer],
            ffn_pieces[layer],
            ffn_plans[layer],
            sides[layer],
            in_cols,
            all_ffn // 3,
        )
        for layer in range(LAYERS)
    ]

    hidden = whole_features(hidden_in)
    grad = whole_features(cotangent)
    stored, summed = [], ()
    for layer in range(LAYERS):
        hidden, summed, saved = layer_forward(
            hidden, summed, params[layer], sizes, (grad,) if layer == 0 else ()
        )
        stored.append(saved)
    hidden_out = hidden + in_order(*summed, row_index & 1, 0).astype(f32)
    hidden_out = own_features(hidden_out.astype(bf16))
    sums, above, waited = [None] * LAYERS, None, ((), (), None)
    heads, taps, input_gains, post_gains = [], [], [], []
    for layer in reversed(range(LAYERS)):
        above, waited, gain_above, post_gain_grad, dheads, dtaps, sums[layer] = layer_backward(
            grad, above, stored[layer], params[layer], sizes, layer, waited
        )
        if gain_above is not None:
            input_gains.insert(0, gain_above[0])
        post_gains.insert(0, post_gain_grad[0])
        heads.insert(0, dheads[:3].reshape(-1))
        taps.insert(0, dtaps[:4].reshape(-1))
    grad, last_gain = last_norm_back(*above)
    input_gains.insert(0, last_gain)
    hidden_grad = own_features(grad.astype(bf16)).astype(f32)
    small = jnp.stack(
        [
            jnp.concatenate(
                [
                    in_blocks(input_gains[layer]),
                    in_blocks(post_gains[layer]),
                    heads[layer],
                    taps[layer],
                ]
            )
            for layer in range(LAYERS)
        ]
    )
    small = sum_small(after(small, sums[0][1]))

    half, wide = gate_weight.shape[2], 2 * gate_weight.shape[2]
    collected, shared_parts = [], []
    for layer in range(LAYERS):
        if layer == LAYERS - 1:
            wide_sum, out_sum = sums[layer]
            whole = jnp.concatenate([wide_sum, sums[0][2], out_sum], axis=1)
            whole = other_half(after(whole, sums[0][3]))
            wide_part, down_part, in_part, shared_part, out_part = jnp.split(
                whole, [wide, wide + half, wide + half + sizes[3], wide + half + in_cols], axis=1
            )
        else:
            wide_sum, mixer_sum = sums[layer][:2]
            whole, mixer = other_half(wide_sum), other_half(mixer_sum)
            wide_part, down_part = whole[:, :wide], whole[:, wide:]
            in_part, shared_part, out_part = jnp.split(mixer, [sizes[3], in_cols], axis=1)
        shared_parts.append(shared_part)
        collected.append((wide_part, in_part, down_part, out_part))

    key_cols = keyval_weight.shape[2]
    placed = []
    for part in shared_parts:
        keyval = jnp.zeros((part.shape[0], key_cols), bf16)
        key_at = state_cols
        keyval = lax.dynamic_update_slice_in_dim(keyval, part[:, key_at : key_at + HEAD], key_first, 1)
        keyval = lax.dynamic_update_slice_in_dim(
            keyval, part[:, key_at + HEAD : key_at + 2 * HEAD], value_first, 1
        )
        key_at = key_at + 2 * HEAD
        steps = lax.dynamic_update_slice_in_dim(
            jnp.zeros((part.shape[0], step_weight.shape[2]), bf16),
            part[:, key_at : key_at + heads_row],
            step_first,
            1,
        )
        total = jnp.concatenate([keyval, part[:, :state_cols], steps], axis=1)
        total = add(total, swap(total, "row", 1))
        placed.append(total.astype(f32) + swap(total, "row", 2).astype(f32))
    features = hidden_in.shape[1]
    width = features * lax.axis_size("col")
    taps = small[:, 2 * width + 3 * LANES :].reshape(LAYERS, 4, input_cols + state_cols)
    heads = small[:, 2 * width : 2 * width + 3 * LANES].reshape(LAYERS, 3, LANES)

    def own_gain(first):
        return lax.dynamic_slice_in_dim(small, first + col_index * features, features, 1)

    def outputs(member, first=None, last=None, turned=False):
        entries = [entry[member].astype(f32) for entry in collected]
        if turned:
            entries = [entry.T[first:last] for entry in entries]
        else:
            entries = [entry[:, first:last] for entry in entries]
        return jnp.stack(entries)

    attn_rows = attention_out.shape[1]
    shared = jnp.stack(placed)
    return (
        hidden_out,
        hidden_grad,
        own_gain(0),
        outputs(1, 0, sizes[1]),
        shared[:, :, :key_cols],
        outputs(1, sizes[1], sizes[2]),
        outputs(1, sizes[2], sizes[3]),
        shared[:, :, key_cols : key_cols + state_cols],
        shared[:, :, key_cols + state_cols :],
        taps[:, :, :input_cols],
        sum_row_small(taps[:, :, input_cols:]),
        heads[:, 0, :heads_row],
        heads[:, 1, :heads_row],
        heads[:, 2, :heads_row],
        outputs(3, 0, attn_rows, True),
        outputs(3, attn_rows, None, True),
        own_gain(width),
        outputs(0, 0, half),
        outputs(0, half, wide),
        outputs(2, 0, None, True),
    )


def solution(mesh):
    placed = (
        P(("dp", "row"), "col"),
        P("dp"),
        P(("dp", "row"), "col"),
        P(None, "col"),
        P(None, "col", "row"),
        P(None, "col", None),
        P(None, "col", "row"),
        P(None, "col", "row"),
        P(None, "col", None),
        P(None, "col", None),
        P(None, None, "row"),
        P(),
        P(None, "row"),
        P(None, "row"),
        P(None, "row"),
        P(None, "row", "col"),
        P(None, "row", "col"),
        P(None, "col"),
        P(None, "col", "row"),
        P(None, "col", "row"),
        P(None, "row", "col"),
    )
    return jax.shard_map(
        shards,
        mesh=mesh,
        in_specs=placed,
        out_specs=(
            P(("dp", "row"), "col"),
            P(("dp", "row"), "col"),
            P(None, "col"),
            P(None, "col", "row"),
            P(None, "col", None),
            P(None, "col", "row"),
            P(None, "col", "row"),
            P(None, "col", None),
            P(None, "col", None),
            P(None, None, "row"),
            P(),
            P(None, "row"),
            P(None, "row"),
            P(None, "row"),
            P(None, "row", "col"),
            P(None, "row", "col"),
            P(None, "col"),
            P(None, "col", "row"),
            P(None, "col", "row"),
            P(None, "row", "col"),
        ),
        check_vma=False,
    )
```
